512 devices in a mesh: dom: 512 (over x, z, y, core).
Axes of the slice: x: 4, y: 8, z: 8, core: 2. Of those that a mesh axis runs over, the one named last changes fastest.
Arguments:
- connectivity: int32 [65536, 64], P('dom'), may hold values from 0 to 4991, as said below
- send_down: int32 [512, 768], P('dom'), may hold values from 0 to 3455, as said below
- send_up: int32 [512, 768], P('dom'), may hold values from 0 to 3455, as said below
- jacobian: float32 [65536], P('dom'), may hold values from 0.5 to 4
- pair_blocks: bfloat16 [131072, 4096], P('dom'), may hold values from -0.75 to 0.75
- pair_target: int32 [131072], P('dom'), may hold values from 0 to 127
- pair_source: int32 [131072], P('dom'), may hold values from 0 to 127
- source_values: bfloat16 [32, 4194304], P(None, 'dom'), may hold values from -6 to 6
Outputs:
- solution: float32 [32, 1769472], P(None, 'dom')
- residual: float32 [32, 1769472], P(None, 'dom')
- new_basis: float32 [32, 1769472], P(None, 'dom')
The draws below stay inside these ranges and needn't reach their ends.
Inputs may be any that keep to these rules, and one draw needn't show every extreme that they name: `connectivity`: slots below 3456 are the partition's own nodes, the next 768 the lower neighbour's send_up list in order, the last 768 the upper neighbour's send_down list in order; the first partition uses no lower slots, the last no upper ones. `send_down`: distinct own node indices in each row. `send_up`: distinct own node indices in each row.
All inputs are finite; a program needn't handle non-finite values.
Results may differ from the reference program's by a relative error of at most 0.0003.
Values sent between devices are 32-bit elements; how exact they have to be, the bound alone decides.
No kernel may reach another device: no remote copies, remote signals or barrier semaphores. Data moves between devices by JAX's collectives and lax.ppermute only.
A program may use at most 64 MiB of HBM per device.

```python
import math
import jax
import jax.numpy as jnp
import numpy as np
from jax import lax

TR = 32
NP = 64
NODE_DEV = 3456
F = 768
E_DEV = 128
E_SRC = 128
P_DEV = 256
DOMAINS = 512
NODES = 1769472
ELEMS = 65536
PAIRS = 131072
SRC_NODES = 4194304


def draw_connectivity(key, part):
    raw = jax.random.randint(key, (ELEMS, NP), 0, NODE_DEV + 2 * F, dtype=jnp.int32)
    device = (jnp.arange(ELEMS, dtype=jnp.int32) // E_DEV)[:, None]
    last_device = ELEMS // E_DEV - 1
    lower = (raw >= NODE_DEV) & (raw < NODE_DEV + F)
    upper = raw >= NODE_DEV + F
    raw = jnp.where((device == 0) & lower, raw - NODE_DEV, raw)
    raw = jnp.where((device == last_device) & upper, raw - NODE_DEV - F, raw)
    return raw.astype(jnp.int32)


def face_lists(key):
    keys = jax.random.split(key, DOMAINS)
    return jax.vmap(lambda single: jax.random.permutation(single, NODE_DEV)[:F])(keys).astype(jnp.int32)


def draw_send_down(key, part):
    return face_lists(jax.random.fold_in(key, 11))


def draw_send_up(key, part):
    return face_lists(jax.random.fold_in(key, 23))


def plant(entries, key, smallest, largest):
    spot = [jax.random.randint(jax.random.fold_in(key, axis), (), 0, length) for axis, length in enumerate(entries.shape)]
    main_axis = entries.shape.index(max(entries.shape))
    beside = spot[:main_axis] + [(spot[main_axis] + 1) % entries.shape[main_axis]] + spot[main_axis + 1:]
    return entries.at[tuple(spot)].set(smallest).at[tuple(beside)].set(largest)


def block_scale(own_key, shape, cuts, low, high):
    def one(position, shards_of):
        steps = jax.random.uniform(jax.random.fold_in(jax.random.fold_in(own_key, 6), position), (shards_of,), jnp.float32, low / len(cuts), high / len(cuts))
        return jnp.repeat(jnp.exp(steps), shape[position] // shards_of).reshape((-1,) + (1,) * (len(shape) - position - 1))

    level = one(*cuts[0])
    for cut in cuts[1:]:
        level = level * one(*cut)
    return level


def gaussian(own_key, dims, spread, bound, pieces=(), kind=jnp.bfloat16):
    values = spread * jax.random.normal(own_key, dims, jnp.float32)
    if pieces:
        values = values * block_scale(own_key, dims, pieces, -0.22, 0.18)
    return jnp.clip(values, -bound, bound).astype(kind)


def setup_inputs(seed: int = 0) -> dict:
    seeds = jax.random.split(jax.random.key(seed), 9)
    return {
        "connectivity": draw_connectivity(jax.random.fold_in(seeds[8], 71), 0),
        "send_down": draw_send_down(jax.random.fold_in(seeds[8], 71), 0),
        "send_up": draw_send_up(jax.random.fold_in(seeds[8], 71), 0),
        "jacobian": jnp.clip(jnp.exp(math.log(4.0) - 2.0794415 * jax.random.uniform(seeds[3], (ELEMS,), jnp.float32) ** block_scale(seeds[3], (ELEMS,), ((0, 512),), -0.2, 0.2)), 0.5, 4.0),
        "pair_blocks": gaussian(seeds[4], (PAIRS, NP * NP), NP ** -0.5, 0.75, ((0, 512),)),
        "pair_target": plant(jax.random.randint(seeds[5], (PAIRS,), 0, E_DEV), jax.random.fold_in(seeds[5], 1), 0, E_DEV - 1).astype(jnp.int32),
        "pair_source": plant(jax.random.randint(seeds[6], (PAIRS,), 0, E_SRC), jax.random.fold_in(seeds[6], 1), 0, E_SRC - 1).astype(jnp.int32),
        "source_values": gaussian(seeds[7], (TR, SRC_NODES), 1.0, 6.0, ((1, 512),)),
    }


line_mass = np.array([[128.0, 99.0, -36.0, 19.0], [99.0, 648.0, -81.0, -36.0], [-36.0, -81.0, 648.0, 99.0], [19.0, -36.0, 99.0, 128.0]]) / 504.0
mass_table = np.kron(np.kron(line_mass, line_mass), line_mass)

def node_ids(connectivity, send_down, send_up):
    count = connectivity.shape[0]
    domains = send_down.shape[0]
    device = (jnp.arange(count, dtype=jnp.int32) // E_DEV)[:, None]
    below = jnp.clip(device - 1, 0, domains - 1)
    above = jnp.clip(device + 1, 0, domains - 1)
    low_slot = jnp.clip(connectivity - NODE_DEV, 0, F - 1)
    high_slot = jnp.clip(connectivity - NODE_DEV - F, 0, F - 1)
    own = device * NODE_DEV + connectivity
    lower = below * NODE_DEV + send_up[below, low_slot]
    upper = above * NODE_DEV + send_down[above, high_slot]
    picked = jnp.where(connectivity < NODE_DEV, own, jnp.where(connectivity < NODE_DEV + F, lower, upper))
    return picked.astype(jnp.int32)

def mass_apply(field, ids, jacobian):
    element_mass = jnp.asarray(mass_table, dtype=field.dtype)
    grouped = ids.reshape(DOMAINS, E_DEV * NP)
    scales = jacobian.reshape(DOMAINS, E_DEV)

    def one_domain(total, item):
        flat, scale = item
        values = field[:, flat].reshape(TR, E_DEV, NP)
        image = jnp.einsum('tep,pq->teq', values, element_mass, precision=lax.Precision.HIGHEST) * scale[None, :, None]
        return (total.at[:, flat].add(image.reshape(TR, E_DEV * NP)), None)
    total, unused = lax.scan(one_domain, jnp.zeros_like(field), (grouped, scales))
    return total

def reference(connectivity, send_down, send_up, jacobian, pair_blocks, pair_target, pair_source, source_values):
    ids = node_ids(connectivity, send_down, send_up)
    grouped_ids = ids.reshape(DOMAINS, E_DEV, NP)
    offsets = jnp.arange(NP, dtype=jnp.int32)

    def one_domain(total, item):
        blocks, target, source, elem_ids, domain = item
        columns = ((domain * E_SRC + source)[:, None] * NP + offsets[None, :]).reshape(-1).astype(jnp.int32)
        values = source_values[:, columns].astype(jnp.float32).reshape(TR, P_DEV, NP)
        mixed = blocks.astype(jnp.float32).reshape(P_DEV, NP, NP)
        contrib = jnp.einsum('pij,tpj->tpi', mixed, values, precision=lax.Precision.HIGHEST)
        targets = elem_ids[target].reshape(-1)
        return (total.at[:, targets].add(contrib.reshape(TR, P_DEV * NP)), None)
    start = jnp.zeros((TR, NODES), jnp.float32)
    items = (pair_blocks.reshape(DOMAINS, P_DEV, NP * NP), pair_target.reshape(DOMAINS, P_DEV), pair_source.reshape(DOMAINS, P_DEV), grouped_ids, jnp.arange(DOMAINS, dtype=jnp.int32))
    right_side, unused = lax.scan(one_domain, start, items)
    high = lax.Precision.HIGHEST
    gram_rhs = jnp.dot(right_side, right_side.T, precision=high)
    lower_rhs = jnp.linalg.cholesky(gram_rhs)
    basis = jax.scipy.linalg.solve_triangular(lower_rhs, right_side, lower=True)
    image = mass_apply(basis, ids, jacobian)
    step_gram = jnp.dot(basis, image.T, precision=high)
    lower_step = jnp.linalg.cholesky(step_gram)
    coeffs = jax.scipy.linalg.cho_solve((lower_step, True), lower_rhs.T).T
    solution = jnp.dot(coeffs, basis, precision=high)
    residual = right_side - jnp.dot(coeffs, image, precision=high)
    lower_new = jnp.linalg.cholesky(jnp.dot(residual, residual.T, precision=high))
    new_basis = jax.scipy.linalg.solve_triangular(lower_new, residual, lower=True)
    return (solution, residual, new_basis)
```

```python
import jax
import jax.numpy as jnp
import numpy as np
from jax import lax
from jax.experimental import pallas as pl
from jax.experimental.pallas import tpu as pltpu
from jax.sharding import Mesh
from jax.sharding import PartitionSpec as P

TR = 32
NODE_DEV = 3456
F = 768
SLOTS = 8192
L = 512
OWN_BLOCKS = 7
HALO_BLOCKS = 3
PAD = OWN_BLOCKS * L - NODE_DEV
BF = jnp.bfloat16
F32 = jnp.float32
I16 = jnp.int16
NT = (((1,), (1,)), ((), ()))
AXES = ("x", "z", "y", "c")
SIZES = {"x": 4, "z": 8, "y": 8, "c": 2}

line_mass = (
    np.array(
        [
            [128.0, 99.0, -36.0, 19.0],
            [99.0, 648.0, -81.0, -36.0],
            [-36.0, -81.0, 648.0, 99.0],
            [19.0, -36.0, 99.0, 128.0],
        ]
    )
    / 504.0
)
mass_table = np.kron(np.kron(line_mass, line_mass), line_mass)


def mass_tiles():
    order = np.arange(64).reshape(32, 2).T.reshape(-1)
    block = mass_table[np.ix_(order, order)].astype(np.float32)
    whole = np.kron(np.eye(4, dtype=np.float32), block)
    high = whole.astype(jnp.bfloat16)
    low = (whole - high.astype(np.float32)).astype(jnp.bfloat16)
    return np.concatenate([high, low], axis=1)


def params(**extra):
    return pltpu.CompilerParams(vmem_limit_bytes=56 * 2**20, **extra)


def vmem(count):
    return [pl.BlockSpec(memory_space=pltpu.VMEM)] * count


def shape(dims, kind=F32):
    return jax.ShapeDtypeStruct(dims, kind)


def aligned(start, size):
    return pl.ds(pl.multiple_of(start, size), size)


def split2(value):
    high = value.astype(BF)
    low = (value - high.astype(F32)).astype(BF)
    return high, low


def one_hot(row):
    spread = jnp.broadcast_to(row.astype(I16), (L, 128))
    index = lax.broadcasted_iota(I16, (L, 128), 0)
    return jnp.where(spread == index, jnp.ones((), BF), jnp.zeros((), BF))


def tiles_of(ids, count):
    blocks = lax.shift_right_logical(ids, 9)
    places = ids & (L - 1)
    hot = jnp.concatenate([one_hot(places[j : j + 1]) for j in range(count)], axis=1)
    return hot, [blocks[j : j + 1] for j in range(count)]


def masked(parts, blocks, first, number):
    out = []
    for j, row in enumerate(blocks):
        here = jnp.broadcast_to(row.astype(I16), (2 * TR, 128))
        tile = parts[:, j * 128 : (j + 1) * 128]
        out.append(
            jnp.concatenate(
                [jnp.where(here == first + b, tile, jnp.zeros((), BF)) for b in range(number)], axis=0
            )
        )
    return jnp.concatenate(out, axis=1)


def picked(rows, blocks, first, number, start):
    out = []
    for j, row in enumerate(blocks):
        here = jnp.broadcast_to(row, (TR, 128))
        tile = start[j]
        for b in range(number):
            tile = jnp.where(here == first + b, rows[b * TR : (b + 1) * TR, j * 128 : (j + 1) * 128], tile)
        out.append(tile)
    return out


def add_scatter(acc, parts, ids, count, first, number):
    hot, blocks = tiles_of(ids, count)
    acc[...] += lax.dot_general(
        masked(parts, blocks, first, number), hot, NT, preferred_element_type=F32
    )


def fold(acc, b):
    return acc[b * 2 * TR : b * 2 * TR + TR] + acc[b * 2 * TR + TR : (b + 1) * 2 * TR]


CHUNK = 2048
TILES = CHUNK // 128
UNROLL = 32


def rhs_kernel(tgt_ref, src_ref, conn_ref, pb_ref, sv_ref, ids_ref, parts_ref, halo_ref, blocks, source, total, wide, acc):
    zero = jnp.zeros((), F32)
    zero16 = jnp.zeros((), BF)
    for g in range(16):
        stack = jnp.concatenate([sv_ref[:, (4 * g + k) * 128 : (4 * g + k + 1) * 128] for k in range(4)], axis=0)
        source[g * 128 : (g + 1) * 128, :] = stack.astype(F32).T.astype(BF)
    @pl.loop(0, 16)
    def _(g):
        for c in range(32):
            rows = pb_ref[aligned(g * 16, 16), c * 128 : (c + 1) * 128].astype(F32)
            blocks[pl.ds(g * 512 + c, 16, stride=32), :] = rows

    conn = conn_ref[...]
    row = lax.broadcasted_iota(jnp.int32, (64, 64), 0)
    col = lax.broadcasted_iota(jnp.int32, (64, 64), 1)
    swap = jnp.where(row == 2 * (col & 31) + lax.shift_right_logical(col, 5), 1.0, 0.0).astype(BF)
    upper = lax.shift_right_logical(conn, 7).astype(F32).astype(BF)
    lower = (conn & 127).astype(F32).astype(BF)
    ids = jnp.dot(upper, swap, preferred_element_type=F32) * 128.0 + jnp.dot(lower, swap, preferred_element_type=F32)
    ids = ids.astype(jnp.int32)
    ids = jnp.where(ids >= NODE_DEV, ids + PAD, ids)
    wide[...] = jnp.concatenate([ids, ids], axis=1)
    lane64 = lax.broadcasted_iota(jnp.int32, (64, 128), 1)
    ids_ref[...] = jnp.where(lane64 < 64, wide[pl.ds(0, 64, stride=2), :], wide[pl.ds(1, 64, stride=2), :])

    total[...] = jnp.zeros_like(total)
    low32 = lax.broadcasted_iota(jnp.int32, (32, 128), 1) < 64
    group = lax.shift_right_logical(lane64, 5).astype(I16)

    @pl.loop(0, 256 // UNROLL)
    def _(i):
        for u in range(UNROLL):
            p = i * UNROLL + u
            s = src_ref[p]
            e = tgt_ref[p]
            k = lax.shift_right_logical(s, 1) & 3
            start = lax.shift_right_logical(s, 3) * 128 + (s & 1) * 64
            value = jnp.where(group == k.astype(I16), source[aligned(start, 64), :], zero16)
            block = blocks[aligned(p * 32, 32), :]
            rows = jnp.concatenate([jnp.where(low32, block, zero), jnp.where(low32, zero, block)], axis=0).astype(BF)
            total[aligned(e * 64, 64), :] += jnp.dot(
                rows, jnp.concatenate([value, value], axis=0), preferred_element_type=F32
            )

    lanes = lax.shift_right_logical(lax.broadcasted_iota(jnp.int32, (128, 128), 1), 5)
    odd = (lanes & 1) == 1
    up = lanes >= 2

    def join(a, b, mask, by):
        return jnp.where(mask, b, a) + pltpu.roll(jnp.where(mask, a, b), by, 1)

    @pl.loop(0, 16, unroll=4)
    def _(g):
        e = [total[aligned(g * 512 + j * 128, 128), :] for j in range(4)]
        both = join(join(e[0], e[1], odd, 32), join(e[2], e[3], odd, 32), up, 64).T
        for j in range(4):
            high, low = split2(both[j * TR : (j + 1) * TR])
            parts_ref[:, aligned(g * 512 + j * 128, 128)] = jnp.concatenate([high, low], axis=0)

    scatter_halo(ids_ref, parts_ref, halo_ref, acc)


def scatter_halo(ids_ref, parts_ref, halo_ref, acc):
    acc[...] = jnp.zeros_like(acc)

    @pl.loop(0, SLOTS // CHUNK)
    def _(k):
        add_scatter(
            acc, parts_ref[:, aligned(k * CHUNK, CHUNK)], ids_ref[aligned(k * TILES, TILES), :], TILES, OWN_BLOCKS, HALO_BLOCKS
        )

    for b in range(HALO_BLOCKS):
        halo_ref[:, b * L : (b + 1) * L] = fold(acc, b)


def right_side_halo(tgt, src, conn, pair_blocks, source_values):
    return pl.pallas_call(
        rhs_kernel,
        out_shape=(shape((64, 128), jnp.int32), shape((2 * TR, SLOTS), BF), shape((TR, 2 * F))),
        in_specs=[pl.BlockSpec(memory_space=pltpu.SMEM)] * 2 + vmem(3),
        out_specs=tuple(vmem(3)),
        scratch_shapes=[
            pltpu.VMEM((8192, 128), F32),
            pltpu.VMEM((2048, 128), BF),
            pltpu.VMEM((8192, 128), F32),
            pltpu.VMEM((128, 128), jnp.int32),
            pltpu.VMEM((HALO_BLOCKS * 2 * TR, L), F32),
        ],
        compiler_params=params(),
        name="rhs",
    )(tgt, src, conn, pair_blocks, source_values)


def own_kernel(ids_ref, parts_ref, out_ref, acc):
    acc[...] = jnp.zeros_like(acc)

    @pl.loop(0, SLOTS // CHUNK)
    def _(k):
        add_scatter(acc, parts_ref[:, aligned(k * CHUNK, CHUNK)], ids_ref[aligned(k * TILES, TILES), :], TILES, 0, OWN_BLOCKS)

    for b in range(OWN_BLOCKS):
        out_ref[:, b * L : (b + 1) * L] = fold(acc, b)


def scatter_own(ids, parts):
    return pl.pallas_call(
        own_kernel,
        out_shape=shape((TR, OWN_BLOCKS * L)),
        in_specs=vmem(2),
        out_specs=vmem(1)[0],
        scratch_shapes=[pltpu.VMEM((OWN_BLOCKS * 2 * TR, L), F32)],
        compiler_params=params(),
        cost_estimate=pl.CostEstimate(flops=2 * 448 * 512 * 8192, bytes_accessed=2**21, transcendentals=0),
        name="own",
    )(ids, parts)


def settle(own_ref, above_ref, below_ref, highs_ref, lows_ref, acc):
    rows = [highs_ref[:, j * 128 : (j + 1) * 128] for j in range(6)] + [lows_ref[:, j * 128 : (j + 1) * 128] for j in range(6)]
    hot = jnp.concatenate([one_hot(r & (L - 1)) for r in rows], axis=1)
    blocks = [lax.shift_right_logical(r, 9) for r in rows]
    high, low = split2(jnp.concatenate([above_ref[...], below_ref[...]], axis=1))
    parts = jnp.concatenate([high, low], axis=0)
    acc[...] = lax.dot_general(masked(parts, blocks, 0, OWN_BLOCKS), hot, NT, preferred_element_type=F32)
    whole = [own_ref[:, b * L : (b + 1) * L] + fold(acc, b) for b in range(OWN_BLOCKS)]
    return whole, hot, blocks


def settle_kernel(own_ref, above_ref, below_ref, highs_ref, lows_ref, out_ref, up_ref, down_ref, table_ref, acc):
    whole, hot, blocks = settle(own_ref, above_ref, below_ref, highs_ref, lows_ref, acc)
    for b, value in enumerate(whole):
        end = min(NODE_DEV, (b + 1) * L)
        out_ref[:, b * L : end] = value[:, : end - b * L]
        high, low = split2(value)
        table_ref[b * TR : (b + 1) * TR, :] = jnp.concatenate([high, low], axis=1)
    rows = jnp.dot(table_ref[...], jnp.concatenate([hot, hot], axis=0), preferred_element_type=F32)
    zeros = [jnp.zeros((TR, 128), F32)] * 12
    values = picked(rows, blocks, 0, OWN_BLOCKS, zeros)
    for j in range(6):
        up_ref[:, j * 128 : (j + 1) * 128] = values[j]
        down_ref[:, j * 128 : (j + 1) * 128] = values[6 + j]


def settle_right(own, above, below, highs, lows):
    return pl.pallas_call(
        settle_kernel,
        out_shape=(
            shape((TR, NODE_DEV)),
            shape((TR, F)),
            shape((TR, F)),
            shape((OWN_BLOCKS * TR, 2 * L), BF),
        ),
        in_specs=vmem(5),
        out_specs=tuple(vmem(4)),
        scratch_shapes=[pltpu.VMEM((OWN_BLOCKS * 2 * TR, L), F32)],
        compiler_params=params(),
        name="settle",
    )(own, above, below, highs, lows)


def gather_kernel(ids_ref, table_ref, jac_ref, out_ref, scale_ref, wide):
    wide[...] = jnp.broadcast_to(jac_ref[...], (128, 128)).T
    lane64 = lax.broadcasted_iota(jnp.int32, (64, 128), 1)
    scale_ref[...] = jnp.where(lane64 < 64, wide[pl.ds(0, 64, stride=2), :], wide[pl.ds(1, 64, stride=2), :])

    @pl.loop(0, SLOTS // CHUNK)
    def _(k):
        hot, blocks = tiles_of(ids_ref[aligned(k * TILES, TILES), :], TILES)
        rows = jnp.dot(table_ref[...], jnp.concatenate([hot, hot], axis=0), preferred_element_type=F32)
        values = picked(rows, blocks, 0, OWN_BLOCKS, [jnp.zeros((TR, 128), F32)] * TILES)
        out_ref[:, aligned(k * CHUNK, CHUNK)] = jnp.concatenate(values, axis=1)


def gather_own(ids, table, jac):
    return pl.pallas_call(
        gather_kernel,
        out_shape=(shape((TR, SLOTS)), shape((64, 128))),
        in_specs=vmem(3),
        out_specs=tuple(vmem(2)),
        scratch_shapes=[pltpu.VMEM((128, 128), F32)],
        compiler_params=params(),
        cost_estimate=pl.CostEstimate(flops=2 * 448 * 512 * 8192, bytes_accessed=2**21, transcendentals=0),
        name="gather",
    )(ids, table, jac)


def mass_kernel(ids_ref, start_ref, below_ref, above_ref, scale_ref, mass_ref, parts_ref, halo_ref, table, acc):
    both = jnp.concatenate([below_ref[...], above_ref[...]], axis=1)
    for b in range(HALO_BLOCKS):
        high, low = split2(both[:, b * L : (b + 1) * L])
        table[b * TR : (b + 1) * TR, :] = jnp.concatenate([high, low], axis=1)
    acc[...] = jnp.zeros_like(acc)

    @pl.loop(0, SLOTS // CHUNK)
    def _(k):
        hot, blocks = tiles_of(ids_ref[aligned(k * TILES, TILES), :], TILES)
        rows = jnp.dot(table[...], jnp.concatenate([hot, hot], axis=0), preferred_element_type=F32)
        start = [start_ref[:, aligned(k * CHUNK + j * 128, 128)] for j in range(TILES)]
        values = picked(rows, blocks, OWN_BLOCKS, HALO_BLOCKS, start)
        split = [split2(jnp.concatenate(values[2 * j : 2 * j + 2], axis=1)) for j in range(TILES // 2)]
        highs = jnp.concatenate([s[0] for s in split], axis=0)
        lows = jnp.concatenate([s[1] for s in split], axis=0)
        image = (
            jnp.dot(highs, mass_ref[:, :256], preferred_element_type=F32)
            + jnp.dot(lows, mass_ref[:, :256], preferred_element_type=F32)
            + jnp.dot(highs, mass_ref[:, 256:], preferred_element_type=F32)
        )
        tiles = []
        scales = scale_ref[aligned(k * TILES, TILES), :]
        for j in range(TILES):
            tile = image[(j // 2) * TR : (j // 2 + 1) * TR, (j % 2) * 128 : (j % 2 + 1) * 128]
            high, low = split2(tile * scales[j : j + 1])
            tiles.append(jnp.concatenate([high, low], axis=0))
        parts = jnp.concatenate(tiles, axis=1)
        parts_ref[:, aligned(k * CHUNK, CHUNK)] = parts
        acc[...] += lax.dot_general(
            masked(parts, blocks, OWN_BLOCKS, HALO_BLOCKS), hot, NT, preferred_element_type=F32
        )

    for b in range(HALO_BLOCKS):
        halo_ref[:, b * L : (b + 1) * L] = fold(acc, b)


def mass_halo(ids, start, below, above, scale, mass):
    return pl.pallas_call(
        mass_kernel,
        out_shape=(shape((2 * TR, SLOTS), BF), shape((TR, 2 * F))),
        in_specs=vmem(6),
        out_specs=tuple(vmem(2)),
        scratch_shapes=[
            pltpu.VMEM((HALO_BLOCKS * TR, 2 * L), BF),
            pltpu.VMEM((HALO_BLOCKS * 2 * TR, L), F32),
        ],
        compiler_params=params(),
        name="mass",
    )(ids, start, below, above, scale, mass)


def lay_flat(square):
    return jnp.concatenate([square[8 * i : 8 * i + 8] for i in range(4)], axis=1)


def lay_square(flat):
    return jnp.concatenate([flat[:, 32 * i : 32 * i + 32] for i in range(4)], axis=0)


def gram_kernel(own_ref, above_ref, below_ref, highs_ref, lows_ref, right_ref, out_ref, gram_ref, acc):
    whole, _, _ = settle(own_ref, above_ref, below_ref, highs_ref, lows_ref, acc)
    for b, value in enumerate(whole):
        end = min(NODE_DEV, (b + 1) * L)
        out_ref[:, b * L : end] = value[:, : end - b * L]
    right = split2(right_ref[...])
    image = split2(out_ref[...])
    stack = jnp.concatenate([right[0], image[0], right[1], image[1]], axis=0)
    full = lax.dot_general(stack, stack, NT, preferred_element_type=F32)
    full = full[:64] + full[64:]
    full = full[:, :64] + full[:, 64:]
    cross = full[:TR, TR:]
    cross = 0.5 * (cross + full[TR:, :TR])
    for i, g in enumerate((full[:TR, :TR], cross, full[TR:, TR:])):
        gram_ref[8 * i : 8 * i + 8, :] = lay_flat(g)


def grams(own, above, below, highs, lows, right):
    return pl.pallas_call(
        gram_kernel,
        out_shape=(shape((TR, NODE_DEV)), shape((24, 128))),
        in_specs=vmem(6),
        out_specs=tuple(vmem(2)),
        scratch_shapes=[pltpu.VMEM((OWN_BLOCKS * 2 * TR, L), F32)],
        compiler_params=params(),
        name="grams",
    )(own, above, below, highs, lows, right)


def hdot(a, b, dims=(((1,), (0,)), ((), ()))):
    return lax.dot_general(a, b, dims, precision=lax.Precision.HIGHEST, preferred_element_type=F32)


def final_kernel(gram_ref, right_ref, image_ref, sol_ref, res_ref, new_ref):
    total = gram_ref[0]
    for i in range(1, gram_ref.shape[0]):
        total = total + gram_ref[i]
    rhs, cross, images = (lay_square(total[8 * i : 8 * i + 8]) for i in range(3))
    row = lax.broadcasted_iota(jnp.int32, (TR, 64), 0)
    col = lax.broadcasted_iota(jnp.int32, (TR, 64), 1)
    cross = 0.5 * (cross + cross.T)

    work = jnp.concatenate([cross, rhs], axis=1)
    for k in range(TR):
        line = work[k : k + 1] * (1.0 / work[k : k + 1, k : k + 1])
        column = jnp.where(row[:, :1] == k, 0.0, work[:, k : k + 1])
        work = jnp.where(row == k, line, work) - column * line
    weights_t = work[:, TR:]
    weights = weights_t.T
    half = hdot(weights, cross)
    gram = rhs - half - half.T + hdot(hdot(weights, images), weights_t)
    gram = 0.5 * (gram + gram.T)

    work = jnp.concatenate([gram, jnp.where(row[:, :TR] == col[:, :TR], 1.0, 0.0)], axis=1)
    for k in range(TR):
        line = work[k : k + 1] * lax.rsqrt(work[k : k + 1, k : k + 1])
        column = work[:, k : k + 1] * lax.rsqrt(work[k : k + 1, k : k + 1])
        column = jnp.where(row[:, :1] > k, column, 0.0)
        work = jnp.where(row == k, line, work) - column * line
    inverse = work[:, TR:]

    mixed = hdot(inverse, weights)
    zero = jnp.zeros((TR, TR), F32)
    eye = jnp.where(row[:, :TR] == col[:, :TR], 1.0, 0.0)
    coeffs = jnp.concatenate(
        [
            jnp.concatenate([weights, zero], axis=1),
            jnp.concatenate([zero, -weights], axis=1),
            jnp.concatenate([inverse, -mixed], axis=1),
        ],
        axis=0,
    )
    high, low = split2(coeffs)
    lhs = jnp.concatenate([high, high, low], axis=1)
    right = right_ref[...]
    rh, rl = split2(right)
    ih, il = split2(image_ref[...])
    stack = jnp.concatenate([rh, ih, rl, il, rh, ih], axis=0)
    out = jnp.dot(lhs, stack, preferred_element_type=F32)
    sol_ref[...] = out[:TR]
    res_ref[...] = right + out[TR : 2 * TR]
    new_ref[...] = out[2 * TR :]


def finish(gram, right, image):
    return pl.pallas_call(
        final_kernel,
        out_shape=(shape((TR, NODE_DEV)),) * 3,
        in_specs=vmem(3),
        out_specs=tuple(vmem(3)),
        compiler_params=params(),
        name="finish",
    )(gram, right, image)


def shifted(value, by):
    pairs = [(i, i + by) for i in range(512) if 0 <= i + by < 512]
    return lax.ppermute(value, AXES, pairs)


def exchanged(value, axes):
    count = int(np.prod([SIZES[a] for a in axes]))
    copies = lax.optimization_barrier(jnp.broadcast_to(value[None], (count,) + value.shape))
    return lax.all_to_all(copies, axes, 0, 0)


def per_device(connectivity, send_down, send_up, jacobian, pair_blocks, pair_target, pair_source, source_values):
    lows = send_down
    highs = send_up
    mass = jnp.asarray(mass_tiles())
    ids, parts, halo = right_side_halo(pair_target, pair_source, connectivity, pair_blocks, source_values)
    above = shifted(halo[:, :F], -1)
    below = shifted(halo[:, F:], 1)
    own = scatter_own(ids, parts)
    right, up, down, table = settle_right(own, above, below, highs, lows)
    below = shifted(up, 1)
    above = shifted(down, -1)
    start, scale = gather_own(ids, table, jacobian[None, :])
    parts, halo = mass_halo(ids, start, below, above, scale, mass)
    above = shifted(halo[:, :F], -1)
    below = shifted(halo[:, F:], 1)
    own = scatter_own(ids, parts)
    image, gram = grams(own, above, below, highs, lows, right)
    gram = exchanged(gram, ("x", "y")).sum(0)
    gram = exchanged(gram, ("z", "c"))
    return finish(gram, right, image)


def solution(mesh):
    mesh = Mesh(mesh.devices.reshape(4, 8, 8, 2), AXES)
    return jax.shard_map(
        per_device,
        mesh=mesh,
        in_specs=(
            P(AXES, None),
            P(AXES, None),
            P(AXES, None),
            P(AXES),
            P(AXES, None),
            P(AXES),
            P(AXES),
            P(None, AXES),
        ),
        out_specs=(P(None, AXES), P(None, AXES), P(None, AXES)),
        check_vma=False,
    )
```

```python
import jax
import jax.numpy as jnp
import numpy as np
from jax import lax
from jax.experimental import pallas as pl
from jax.experimental.pallas import tpu as pltpu
from jax.sharding import Mesh
from jax.sharding import PartitionSpec as P

TR = 32
NODE_DEV = 3456
F = 768
SLOTS = 8192
L = 512
OWN_BLOCKS = 7
HALO_BLOCKS = 3
PAD = OWN_BLOCKS * L - NODE_DEV
BF = jnp.bfloat16
F32 = jnp.float32
I16 = jnp.int16
NT = (((1,), (1,)), ((), ()))
AXES = ("x", "z", "y", "c")
SIZES = {"x": 4, "z": 8, "y": 8, "c": 2}

line_mass = (
    np.array(
        [
            [128.0, 99.0, -36.0, 19.0],
            [99.0, 648.0, -81.0, -36.0],
            [-36.0, -81.0, 648.0, 99.0],
            [19.0, -36.0, 99.0, 128.0],
        ]
    )
    / 504.0
)
mass_table = np.kron(np.kron(line_mass, line_mass), line_mass)


def mass_tiles():
    order = np.arange(64).reshape(32, 2).T.reshape(-1)
    block = mass_table[np.ix_(order, order)].astype(np.float32)
    whole = np.kron(np.eye(4, dtype=np.float32), block)
    high = whole.astype(jnp.bfloat16)
    low = (whole - high.astype(np.float32)).astype(jnp.bfloat16)
    return np.concatenate([high, low], axis=1)


def params(mebibytes=24):
    return pltpu.CompilerParams(vmem_limit_bytes=mebibytes * 2**20)


def vmem(count):
    return [pl.BlockSpec(memory_space=pltpu.VMEM)] * count


def hbm(count):
    return [pl.BlockSpec(memory_space=pltpu.MemorySpace.HBM)] * count


def shape(dims, kind=F32):
    return jax.ShapeDtypeStruct(dims, kind)


def aligned(start, size):
    return pl.ds(pl.multiple_of(start, size), size)


def split2(value):
    high = value.astype(BF)
    low = (value - high.astype(F32)).astype(BF)
    return high, low


def one_hot(row):
    spread = jnp.broadcast_to(row.astype(I16), (L, 128))
    index = lax.broadcasted_iota(I16, (L, 128), 0)
    return jnp.where(spread == index, jnp.ones((), BF), jnp.zeros((), BF))


def tiles_of(ids, count):
    blocks = lax.shift_right_logical(ids, 9)
    places = ids & (L - 1)
    hot = jnp.concatenate([one_hot(places[j : j + 1]) for j in range(count)], axis=1)
    return hot, [blocks[j : j + 1] for j in range(count)]


def masked(parts, blocks, first, number):
    out = []
    for j, row in enumerate(blocks):
        here = jnp.broadcast_to(row.astype(I16), (2 * TR, 128))
        tile = parts[:, j * 128 : (j + 1) * 128]
        out.append(
            jnp.concatenate(
                [jnp.where(here == first + b, tile, jnp.zeros((), BF)) for b in range(number)], axis=0
            )
        )
    return jnp.concatenate(out, axis=1)


def picked(rows, blocks, first, number, start):
    out = []
    for j, row in enumerate(blocks):
        here = jnp.broadcast_to(row, (TR, 128))
        tile = start[j]
        for b in range(number):
            tile = jnp.where(here == first + b, rows[b * TR : (b + 1) * TR, j * 128 : (j + 1) * 128], tile)
        out.append(tile)
    return out


def add_scatter(acc, parts, ids, count, first, number):
    hot, blocks = tiles_of(ids, count)
    acc[...] += lax.dot_general(
        masked(parts, blocks, first, number), hot, NT, preferred_element_type=F32
    )


def fold(acc, b):
    return acc[b * 2 * TR : b * 2 * TR + TR] + acc[b * 2 * TR + TR : (b + 1) * 2 * TR]


CHUNK = 2048
TILES = CHUNK // 128
UNROLL = 128


def rhs_kernel(
    tgt_hbm,
    src_hbm,
    conn_hbm,
    pb_hbm,
    sv_hbm,
    ids_hbm,
    parts_hbm,
    low_ref,
    high_ref,
    tgt_ref,
    src_ref,
    conn_ref,
    pb_ref,
    sv_ref,
    ids_ref,
    parts_ref,
    blocks,
    source,
    total,
    wide,
    acc,
    sems,
):
    zero = jnp.zeros((), F32)
    zero16 = jnp.zeros((), BF)
    small = [
        pltpu.make_async_copy(a, b, sems.at[i])
        for i, (a, b) in enumerate(((sv_hbm, sv_ref), (conn_hbm, conn_ref), (tgt_hbm, tgt_ref), (src_hbm, src_ref)))
    ]
    large = [
        pltpu.make_async_copy(pb_hbm.at[pl.ds(64 * i, 64), :], pb_ref.at[pl.ds(64 * i, 64), :], sems.at[4 + i]) for i in range(4)
    ]
    for copy in small + large:
        copy.start()
    total[...] = jnp.zeros_like(total)
    small[0].wait()
    for g in range(16):
        stack = jnp.concatenate([sv_ref[:, (4 * g + k) * 128 : (4 * g + k + 1) * 128] for k in range(4)], axis=0)
        source[g * 128 : (g + 1) * 128, :] = stack.astype(F32).T.astype(BF)
    for copy in small[1:]:
        copy.wait()
    for i in range(4):
        large[i].wait()

        @pl.loop(4 * i, 4 * i + 4)
        def _(g):
            for c in range(32):
                rows = pb_ref[aligned(g * 16, 16), c * 128 : (c + 1) * 128].astype(F32)
                blocks[pl.ds(g * 528 + c, 16, stride=33), :] = rows

    conn = conn_ref[...].astype(F32).T.astype(jnp.int32)
    row = lax.broadcasted_iota(jnp.int32, (64, 64), 0)
    col = lax.broadcasted_iota(jnp.int32, (64, 64), 1)
    swap = jnp.where(row == 2 * (col & 31) + lax.shift_right_logical(col, 5), 1.0, 0.0).astype(BF)
    upper = lax.shift_right_logical(conn, 7).astype(F32).astype(BF)
    lower = (conn & 127).astype(F32).astype(BF)
    ids = jnp.dot(upper, swap, preferred_element_type=F32) * 128.0 + jnp.dot(lower, swap, preferred_element_type=F32)
    ids = ids.astype(jnp.int32)
    ids = jnp.where(ids >= NODE_DEV, ids + PAD, ids)
    wide[...] = jnp.concatenate([ids, ids], axis=1)
    lane64 = lax.broadcasted_iota(jnp.int32, (64, 128), 1)
    ids_ref[...] = jnp.where(lane64 < 64, wide[pl.ds(0, 64, stride=2), :], wide[pl.ds(1, 64, stride=2), :])

    low32 = lax.broadcasted_iota(jnp.int32, (32, 128), 1) < 64
    group = lax.shift_right_logical(lane64, 5).astype(I16)

    @pl.loop(0, 256 // UNROLL)
    def _(i):
        for u in range(UNROLL):
            p = i * UNROLL + u
            s = src_ref[p]
            e = tgt_ref[p]
            k = lax.shift_right_logical(s, 1) & 3
            start = lax.shift_right_logical(s, 3) * 128 + (s & 1) * 64
            value = jnp.where(group == k.astype(I16), source[aligned(start, 64), :], zero16)
            block = blocks[pl.ds(p * 33,32), :]
            rows = jnp.concatenate([jnp.where(low32, block, zero), jnp.where(low32, zero, block)], axis=0).astype(BF)
            total[aligned(e * 64, 64), :] += jnp.dot(
                rows, jnp.concatenate([value, value], axis=0), preferred_element_type=F32
            )

    lanes = lax.shift_right_logical(lax.broadcasted_iota(jnp.int32, (128, 128), 1), 5)
    odd = (lanes & 1) == 1
    up = lanes >= 2

    def join(a, b, mask, by):
        return jnp.where(mask, b, a) + pltpu.roll(jnp.where(mask, a, b), by, 1)

    @pl.loop(0, 16, unroll=True)
    def _(g):
        e = [total[aligned(g * 512 + j * 128, 128), :] for j in range(4)]
        both = join(join(e[0], e[1], odd, 32), join(e[2], e[3], odd, 32), up, 64).T
        for j in range(4):
            high, low = split2(both[j * TR : (j + 1) * TR])
            parts_ref[:, aligned(g * 512 + j * 128, 128)] = jnp.concatenate([high, low], axis=0)

    results = [
        pltpu.make_async_copy(a, b, sems.at[8 + i]) for i, (a, b) in enumerate(((ids_ref, ids_hbm), (parts_ref, parts_hbm)))
    ]
    for copy in results:
        copy.start()
    scatter_halo(ids_ref, parts_ref, acc)
    halves(acc, low_ref, high_ref)
    for copy in results:
        copy.wait()


def scatter_halo(ids_ref, parts_ref, acc):
    acc[...] = jnp.zeros_like(acc)

    @pl.loop(0, SLOTS // CHUNK, unroll=True)
    def _(k):
        add_scatter(
            acc, parts_ref[:, aligned(k * CHUNK, CHUNK)], ids_ref[aligned(k * TILES, TILES), :], TILES, OWN_BLOCKS, HALO_BLOCKS
        )


def halves(acc, low_ref, high_ref):
    first, middle, last = (fold(acc, b) for b in range(HALO_BLOCKS))
    low_ref[:, :L] = first
    low_ref[:, L:] = middle[:, : F - L]
    high_ref[:, : F - L] = middle[:, F - L :]
    high_ref[:, F - L :] = last


def right_side_halo(tgt, src, conn, pair_blocks, source_values):
    return pl.pallas_call(
        rhs_kernel,
        out_shape=(shape((64, 128), jnp.int32), shape((2 * TR, SLOTS), BF), shape((TR, F)), shape((TR, F))),
        in_specs=hbm(5),
        out_specs=tuple(hbm(2) + vmem(2)),
        scratch_shapes=[
            pltpu.SMEM((256,), jnp.int32),
            pltpu.SMEM((256,), jnp.int32),
            pltpu.VMEM((64, 128), jnp.int32),
            pltpu.VMEM((256, 4096), BF),
            pltpu.VMEM((TR, SLOTS), BF),
            pltpu.VMEM((64, 128), jnp.int32),
            pltpu.VMEM((2 * TR, SLOTS), BF),
            pltpu.VMEM((8448, 128), F32),
            pltpu.VMEM((2048, 128), BF),
            pltpu.VMEM((8192, 128), F32),
            pltpu.VMEM((128, 128), jnp.int32),
            pltpu.VMEM((HALO_BLOCKS * 2 * TR, L), F32),
            pltpu.SemaphoreType.DMA((10,)),
        ],
        compiler_params=params(54),
        name="rhs",
    )(tgt, src, conn, pair_blocks, source_values)


def own_kernel(ids_ref, parts_ref, out_ref, acc):
    acc[...] = jnp.zeros_like(acc)

    @pl.loop(0, SLOTS // CHUNK, unroll=True)
    def _(k):
        add_scatter(acc, parts_ref[:, aligned(k * CHUNK, CHUNK)], ids_ref[aligned(k * TILES, TILES), :], TILES, 0, OWN_BLOCKS)

    for b in range(OWN_BLOCKS):
        out_ref[:, b * L : (b + 1) * L] = fold(acc, b)


def scatter_own(ids, parts):
    return pl.pallas_call(
        own_kernel,
        out_shape=shape((TR, OWN_BLOCKS * L)),
        in_specs=vmem(2),
        out_specs=vmem(1)[0],
        scratch_shapes=[pltpu.VMEM((OWN_BLOCKS * 2 * TR, L), F32)],
        compiler_params=params(),
        cost_estimate=pl.CostEstimate(flops=2 * 448 * 512 * 8192, bytes_accessed=2**21, transcendentals=0),
        name="own",
    )(ids, parts)


def settle(own_ref, above_ref, below_ref, highs_ref, lows_ref, acc):
    rows = [highs_ref[:, j * 128 : (j + 1) * 128] for j in range(6)] + [lows_ref[:, j * 128 : (j + 1) * 128] for j in range(6)]
    hot = jnp.concatenate([one_hot(r & (L - 1)) for r in rows], axis=1)
    blocks = [lax.shift_right_logical(r, 9) for r in rows]
    high, low = split2(jnp.concatenate([above_ref[...], below_ref[...]], axis=1))
    parts = jnp.concatenate([high, low], axis=0)
    acc[...] = lax.dot_general(masked(parts, blocks, 0, OWN_BLOCKS), hot, NT, preferred_element_type=F32)
    whole = [own_ref[:, b * L : (b + 1) * L] + fold(acc, b) for b in range(OWN_BLOCKS)]
    return whole, hot, blocks


def settle_kernel(own_ref, above_ref, below_ref, highs_ref, lows_ref, out_ref, up_ref, down_ref, table_ref, acc):
    whole, hot, blocks = settle(own_ref, above_ref, below_ref, highs_ref, lows_ref, acc)
    for b, value in enumerate(whole):
        end = min(NODE_DEV, (b + 1) * L)
        out_ref[:, b * L : end] = value[:, : end - b * L]
        high, low = split2(value)
        table_ref[b * TR : (b + 1) * TR, :] = jnp.concatenate([high, low], axis=1)
    rows = jnp.dot(table_ref[...], jnp.concatenate([hot, hot], axis=0), preferred_element_type=F32)
    zeros = [jnp.zeros((TR, 128), F32)] * 12
    values = picked(rows, blocks, 0, OWN_BLOCKS, zeros)
    for j in range(6):
        up_ref[:, j * 128 : (j + 1) * 128] = values[j]
        down_ref[:, j * 128 : (j + 1) * 128] = values[6 + j]


def settle_right(own, above, below, highs, lows):
    return pl.pallas_call(
        settle_kernel,
        out_shape=(
            shape((TR, NODE_DEV)),
            shape((TR, F)),
            shape((TR, F)),
            shape((OWN_BLOCKS * TR, 2 * L), BF),
        ),
        in_specs=vmem(5),
        out_specs=tuple(vmem(4)),
        scratch_shapes=[pltpu.VMEM((OWN_BLOCKS * 2 * TR, L), F32)],
        compiler_params=params(),
        name="settle",
    )(own, above, below, highs, lows)


def gather_kernel(ids_ref, table_ref, jac_ref, out_ref, scale_ref, wide):
    wide[...] = jnp.broadcast_to(jac_ref[...], (128, 128)).T
    lane64 = lax.broadcasted_iota(jnp.int32, (64, 128), 1)
    scale_ref[...] = jnp.where(lane64 < 64, wide[pl.ds(0, 64, stride=2), :], wide[pl.ds(1, 64, stride=2), :])

    @pl.loop(0, SLOTS // CHUNK, unroll=True)
    def _(k):
        hot, blocks = tiles_of(ids_ref[aligned(k * TILES, TILES), :], TILES)
        rows = jnp.dot(table_ref[...], jnp.concatenate([hot, hot], axis=0), preferred_element_type=F32)
        values = picked(rows, blocks, 0, OWN_BLOCKS, [jnp.zeros((TR, 128), F32)] * TILES)
        out_ref[:, aligned(k * CHUNK, CHUNK)] = jnp.concatenate(values, axis=1)


def gather_own(ids, table, jac):
    return pl.pallas_call(
        gather_kernel,
        out_shape=(shape((TR, SLOTS)), shape((64, 128))),
        in_specs=vmem(3),
        out_specs=tuple(vmem(2)),
        scratch_shapes=[pltpu.VMEM((128, 128), F32)],
        compiler_params=params(),
        cost_estimate=pl.CostEstimate(flops=2 * 448 * 512 * 8192, bytes_accessed=2**21, transcendentals=0),
        name="gather",
    )(ids, table, jac)


def mass_kernel(ids_ref, start_ref, below_ref, above_ref, scale_ref, mass_ref, parts_ref, low_ref, high_ref, table, acc):
    both = jnp.concatenate([below_ref[...], above_ref[...]], axis=1)
    for b in range(HALO_BLOCKS):
        high, low = split2(both[:, b * L : (b + 1) * L])
        table[b * TR : (b + 1) * TR, :] = jnp.concatenate([high, low], axis=1)
    acc[...] = jnp.zeros_like(acc)

    @pl.loop(0, SLOTS // CHUNK, unroll=True)
    def _(k):
        hot, blocks = tiles_of(ids_ref[aligned(k * TILES, TILES), :], TILES)
        rows = jnp.dot(table[...], jnp.concatenate([hot, hot], axis=0), preferred_element_type=F32)
        start = [start_ref[:, aligned(k * CHUNK + j * 128, 128)] for j in range(TILES)]
        values = picked(rows, blocks, OWN_BLOCKS, HALO_BLOCKS, start)
        split = [split2(jnp.concatenate(values[2 * j : 2 * j + 2], axis=1)) for j in range(TILES // 2)]
        highs = jnp.concatenate([s[0] for s in split], axis=0)
        lows = jnp.concatenate([s[1] for s in split], axis=0)
        image = (
            jnp.dot(highs, mass_ref[:, :256], preferred_element_type=F32)
            + jnp.dot(lows, mass_ref[:, :256], preferred_element_type=F32)
            + jnp.dot(highs, mass_ref[:, 256:], preferred_element_type=F32)
        )
        tiles = []
        scales = scale_ref[aligned(k * TILES, TILES), :]
        for j in range(TILES):
            tile = image[(j // 2) * TR : (j // 2 + 1) * TR, (j % 2) * 128 : (j % 2 + 1) * 128]
            high, low = split2(tile * scales[j : j + 1])
            tiles.append(jnp.concatenate([high, low], axis=0))
        parts = jnp.concatenate(tiles, axis=1)
        parts_ref[:, aligned(k * CHUNK, CHUNK)] = parts
        acc[...] += lax.dot_general(
            masked(parts, blocks, OWN_BLOCKS, HALO_BLOCKS), hot, NT, preferred_element_type=F32
        )

    halves(acc, low_ref, high_ref)


def mass_halo(ids, start, below, above, scale, mass):
    return pl.pallas_call(
        mass_kernel,
        out_shape=(shape((2 * TR, SLOTS), BF), shape((TR, F)), shape((TR, F))),
        in_specs=vmem(6),
        out_specs=tuple(vmem(3)),
        scratch_shapes=[
            pltpu.VMEM((HALO_BLOCKS * TR, 2 * L), BF),
            pltpu.VMEM((HALO_BLOCKS * 2 * TR, L), F32),
        ],
        compiler_params=params(),
        name="mass",
    )(ids, start, below, above, scale, mass)


def places():
    return tuple(lax.broadcasted_iota(jnp.int32, (TR, TR), i) for i in range(2))


def lay_flat(square):
    return jnp.concatenate([square[8 * i : 8 * i + 8] for i in range(4)], axis=1)


def lay_square(flat):
    return jnp.concatenate([flat[:, 32 * i : 32 * i + 32] for i in range(4)], axis=0)


def gram_kernel(own_ref, above_ref, below_ref, highs_ref, lows_ref, right_ref, out_ref, gram_ref, acc):
    whole, _, _ = settle(own_ref, above_ref, below_ref, highs_ref, lows_ref, acc)
    for b, value in enumerate(whole):
        end = min(NODE_DEV, (b + 1) * L)
        out_ref[:, b * L : end] = value[:, : end - b * L]
    right = split2(right_ref[...])
    image = split2(out_ref[...])
    stack = jnp.concatenate([right[0], image[0], right[1], image[1]], axis=0)
    full = lax.dot_general(stack, stack, NT, preferred_element_type=F32)
    full = full[:64] + full[64:]
    full = full[:, :64] + full[:, 64:]
    cross = full[:TR, TR:]
    cross = 0.5 * (cross + full[TR:, :TR])
    rhs, images = full[:TR, :TR], full[TR:, TR:]
    row, col = places()
    diagonal = jnp.sum(jnp.where(row == col, images, 0.0), axis=0, keepdims=True)
    first = jnp.where(row >= col, rhs, images)
    second = jnp.where(row == 0, diagonal, images[:1, :1])
    gram_ref[0:8, :] = lay_flat(first)
    gram_ref[8:16, :] = lay_flat(jnp.where(row >= col, cross, second))


def grams(own, above, below, highs, lows, right):
    return pl.pallas_call(
        gram_kernel,
        out_shape=(shape((TR, NODE_DEV)), shape((16, 128))),
        in_specs=vmem(6),
        out_specs=tuple(vmem(2)),
        scratch_shapes=[pltpu.VMEM((OWN_BLOCKS * 2 * TR, L), F32)],
        compiler_params=params(),
        name="grams",
    )(own, above, below, highs, lows, right)


def hdot(a, b, dims=(((1,), (0,)), ((), ()))):
    return lax.dot_general(a, b, dims, precision=lax.Precision.HIGHEST, preferred_element_type=F32)


def eliminate(work, above):
    groups = TR // 8
    row = lax.broadcasted_iota(jnp.int32, (8, 128), 0)
    work = [work[8 * g : 8 * g + 8] for g in range(groups)]
    scale = [jnp.zeros((8, 128), F32)] * groups
    for panel in range(groups):
        columns = {
            k: [jnp.broadcast_to(work[g][:, k : k + 1], (8, 128)) for g in range(groups)]
            for k in range(8 * panel, 8 * panel + 8)
        }
        for k in range(8 * panel, 8 * panel + 8):
            g0, r = divmod(k, 8)
            column = columns[k]
            pivot = column[g0][r : r + 1]
            inverse = 1.0 / pivot
            if not above:
                scale[g0] = jnp.where(row == r, jnp.broadcast_to(pivot, (8, 128)), scale[g0])

            def update(target):
                line = jnp.broadcast_to(target[g0][r : r + 1] * inverse, (8, 128))
                out = []
                for g in range(groups):
                    if g < g0 and not above:
                        out.append(target[g])
                    elif g == g0:
                        less = target[g] - column[g] * line
                        if above:
                            out.append(jnp.where(row == r, line, less))
                        else:
                            out.append(jnp.where(row > r, less, target[g]))
                    else:
                        out.append(target[g] - column[g] * line)
                return out

            work = update(work)
            for j in range(k + 1, 8 * panel + 8):
                columns[j] = update(columns[j])
    if not above:
        work = [w * lax.rsqrt(s) for w, s in zip(work, scale)]
    return jnp.concatenate(work, axis=0)


def final_kernel(gram_ref, right_ref, image_ref, sol_ref, res_ref, new_ref):
    total = gram_ref[0]
    for i in range(1, gram_ref.shape[0]):
        total = total + gram_ref[i]
    first = lay_square(total[:8])
    second = lay_square(total[8:])
    first_t = first.T
    second_t = second.T
    row, col = places()
    rhs = jnp.where(row >= col, first, first_t)
    cross = jnp.where(row >= col, second, second_t)
    diagonal = jnp.where(col == 0, second[1:2, 2:3], second[:1, :])
    images = jnp.where(row < col, first, jnp.where(row == col, diagonal, first_t))
    zero = jnp.zeros((TR, TR), F32)
    eye = jnp.where(row == col, 1.0, 0.0)

    weights_t = eliminate(jnp.concatenate([cross, rhs, zero, zero], axis=1), True)[:, TR : 2 * TR]
    weights = weights_t.T
    both = hdot(weights, jnp.concatenate([cross, images], axis=1))
    gram = rhs - 2.0 * both[:, :TR] + hdot(both[:, TR:], weights_t)
    work = eliminate(jnp.concatenate([gram, eye, weights, zero], axis=1), False)
    inverse = work[:, TR : 2 * TR]
    mixed = work[:, 2 * TR : 3 * TR]
    coeffs = jnp.concatenate(
        [
            jnp.concatenate([weights, zero], axis=1),
            jnp.concatenate([zero, -weights], axis=1),
            jnp.concatenate([inverse, -mixed], axis=1),
        ],
        axis=0,
    )
    high, low = split2(coeffs)
    right = right_ref[...]
    rh, rl = split2(right)
    ih, il = split2(image_ref[...])
    highs = jnp.concatenate([rh, ih], axis=0)
    lows = jnp.concatenate([rl, il], axis=0)
    out = (
        jnp.dot(high, highs, preferred_element_type=F32)
        + jnp.dot(high, lows, preferred_element_type=F32)
        + jnp.dot(low, highs, preferred_element_type=F32)
    )
    sol_ref[...] = out[:TR]
    res_ref[...] = right + out[TR : 2 * TR]
    new_ref[...] = out[2 * TR :]


def finish(gram, right, image):
    return pl.pallas_call(
        final_kernel,
        out_shape=(shape((TR, NODE_DEV)),) * 3,
        in_specs=vmem(3),
        out_specs=tuple(vmem(3)),
        compiler_params=params(),
        name="finish",
    )(gram, right, image)


def shifted(value, by):
    pairs = [(i, i + by) for i in range(512) if 0 <= i + by < 512]
    return lax.ppermute(value, AXES, pairs)


def exchanged(value, axes):
    count = int(np.prod([SIZES[a] for a in axes]))
    copies = lax.optimization_barrier(jnp.broadcast_to(value[None], (count,) + value.shape))
    return lax.all_to_all(copies, axes, 0, 0)


def per_device(connectivity, send_down, send_up, jacobian, pair_blocks, pair_target, pair_source, source_values):
    lows = send_down
    highs = send_up
    mass = jnp.asarray(mass_tiles())
    ids, parts, low, high = right_side_halo(pair_target, pair_source, connectivity.T, pair_blocks, source_values)
    above = shifted(low, -1)
    below = shifted(high, 1)
    own = scatter_own(ids, parts)
    right, up, down, table = settle_right(own, above, below, highs, lows)
    below = shifted(up, 1)
    above = shifted(down, -1)
    start, scale = gather_own(ids, table, jacobian[None, :])
    parts, low, high = mass_halo(ids, start, below, above, scale, mass)
    above = shifted(low, -1)
    below = shifted(high, 1)
    own = scatter_own(ids, parts)
    image, gram = grams(own, above, below, highs, lows, right)
    gram = exchanged(gram, ("x", "y")).sum(0)
    gram = exchanged(gram, ("z", "c"))
    return finish(gram, right, image)


def solution(mesh):
    mesh = Mesh(mesh.devices.reshape(4, 8, 8, 2), AXES)
    return jax.shard_map(
        per_device,
        mesh=mesh,
        in_specs=(
            P(AXES, None),
            P(AXES, None),
            P(AXES, None),
            P(AXES),
            P(AXES, None),
            P(AXES),
            P(AXES),
            P(None, AXES),
        ),
        out_specs=(P(None, AXES), P(None, AXES), P(None, AXES)),
        check_vma=False,
    )
```

```python
import jax
import jax.numpy as jnp
import numpy as np
from jax import lax
from jax.experimental import pallas as pl
from jax.experimental.pallas import tpu as pltpu
from jax.sharding import Mesh
from jax.sharding import PartitionSpec as P

TR = 32
NODE_DEV = 3456
F = 768
SLOTS = 8192
L = 512
OWN_BLOCKS = 7
HALO_BLOCKS = 3
PAD = OWN_BLOCKS * L - NODE_DEV
BF = jnp.bfloat16
F32 = jnp.float32
I16 = jnp.int16
NT = (((1,), (1,)), ((), ()))
AXES = ("x", "z", "y", "c")
SIZES = {"x": 4, "z": 8, "y": 8, "c": 2}

line_mass = (
    np.array(
        [
            [128.0, 99.0, -36.0, 19.0],
            [99.0, 648.0, -81.0, -36.0],
            [-36.0, -81.0, 648.0, 99.0],
            [19.0, -36.0, 99.0, 128.0],
        ]
    )
    / 504.0
)
mass_table = np.kron(np.kron(line_mass, line_mass), line_mass)


def mass_tiles():
    order = np.arange(64).reshape(32, 2).T.reshape(-1)
    block = mass_table[np.ix_(order, order)].astype(np.float32)
    whole = np.kron(np.eye(4, dtype=np.float32), block)
    high = whole.astype(jnp.bfloat16)
    low = (whole - high.astype(np.float32)).astype(jnp.bfloat16)
    return np.concatenate([high, low], axis=1)


def params(mebibytes=24):
    return pltpu.CompilerParams(vmem_limit_bytes=mebibytes * 2**20)


def vmem(count):
    return [pl.BlockSpec(memory_space=pltpu.VMEM)] * count


def hbm(count):
    return [pl.BlockSpec(memory_space=pltpu.MemorySpace.HBM)] * count


def shape(dims, kind=F32):
    return jax.ShapeDtypeStruct(dims, kind)


def aligned(start, size):
    return pl.ds(pl.multiple_of(start, size), size)


def split2(value):
    high = value.astype(BF)
    low = (value - high.astype(F32)).astype(BF)
    return high, low


def one_hot(row):
    spread = jnp.broadcast_to(row.astype(I16), (L, 128))
    index = lax.broadcasted_iota(I16, (L, 128), 0)
    return jnp.where(spread == index, jnp.ones((), BF), jnp.zeros((), BF))


def tiles_of(ids, count):
    blocks = lax.shift_right_logical(ids, 9)
    places = ids & (L - 1)
    hot = jnp.concatenate([one_hot(places[j : j + 1]) for j in range(count)], axis=1)
    return hot, [blocks[j : j + 1] for j in range(count)]


def masked(parts, blocks, first, number):
    out = []
    for j, row in enumerate(blocks):
        here = jnp.broadcast_to(row.astype(I16), (2 * TR, 128))
        tile = parts[:, j * 128 : (j + 1) * 128]
        out.append(
            jnp.concatenate(
                [jnp.where(here == first + b, tile, jnp.zeros((), BF)) for b in range(number)], axis=0
            )
        )
    return jnp.concatenate(out, axis=1)


def picked(rows, blocks, first, number, start):
    out = []
    for j, row in enumerate(blocks):
        tile = start[j]
        height = tile.shape[0]
        here = jnp.broadcast_to(row, (height, 128))
        for b in range(number):
            tile = jnp.where(here == first + b, rows[b * height : (b + 1) * height, j * 128 : (j + 1) * 128], tile)
        out.append(tile)
    return out


def add_scatter(acc, parts, ids, count, first, number):
    hot, blocks = tiles_of(ids, count)
    acc[...] += lax.dot_general(
        masked(parts, blocks, first, number), hot, NT, preferred_element_type=F32
    )


def fold(acc, b):
    return acc[b * 2 * TR : b * 2 * TR + TR] + acc[b * 2 * TR + TR : (b + 1) * 2 * TR]


CHUNK = 2048
TILES = CHUNK // 128
UNROLL = 128


def rhs_kernel(
    tgt_hbm,
    src_hbm,
    conn_hbm,
    pb_hbm,
    sv_hbm,
    ids_hbm,
    parts_hbm,
    near_ref,
    far_ref,
    tgt_ref,
    src_ref,
    conn_ref,
    pb_ref,
    sv_ref,
    ids_ref,
    parts_ref,
    blocks,
    source,
    total,
    wide,
    acc,
    sems,
):
    zero = jnp.zeros((), F32)
    zero16 = jnp.zeros((), BF)
    small = [
        pltpu.make_async_copy(a, b, sems.at[i])
        for i, (a, b) in enumerate(((sv_hbm, sv_ref), (conn_hbm, conn_ref), (tgt_hbm, tgt_ref), (src_hbm, src_ref)))
    ]
    large = [
        pltpu.make_async_copy(pb_hbm.at[pl.ds(64 * i, 64), :], pb_ref.at[pl.ds(64 * i, 64), :], sems.at[4 + i]) for i in range(4)
    ]
    for copy in small + large:
        copy.start()
    total[...] = jnp.zeros_like(total)
    small[0].wait()
    for g in range(16):
        stack = jnp.concatenate([sv_ref[:, (4 * g + k) * 128 : (4 * g + k + 1) * 128] for k in range(4)], axis=0)
        source[g * 128 : (g + 1) * 128, :] = stack.astype(F32).T.astype(BF)
    for copy in small[1:]:
        copy.wait()
    for i in range(4):
        large[i].wait()

        @pl.loop(4 * i, 4 * i + 4)
        def _(g):
            for c in range(32):
                rows = pb_ref[aligned(g * 16, 16), c * 128 : (c + 1) * 128].astype(F32)
                blocks[pl.ds(g * 528 + c, 16, stride=33), :] = rows

    conn = conn_ref[...].astype(F32).T.astype(jnp.int32)
    row = lax.broadcasted_iota(jnp.int32, (64, 64), 0)
    col = lax.broadcasted_iota(jnp.int32, (64, 64), 1)
    swap = jnp.where(row == 2 * (col & 31) + lax.shift_right_logical(col, 5), 1.0, 0.0).astype(BF)
    upper = lax.shift_right_logical(conn, 7).astype(F32).astype(BF)
    lower = (conn & 127).astype(F32).astype(BF)
    ids = jnp.dot(upper, swap, preferred_element_type=F32) * 128.0 + jnp.dot(lower, swap, preferred_element_type=F32)
    ids = ids.astype(jnp.int32)
    ids = jnp.where(ids >= NODE_DEV, ids + PAD, ids)
    wide[...] = jnp.concatenate([ids, ids], axis=1)
    lane64 = lax.broadcasted_iota(jnp.int32, (64, 128), 1)
    ids_ref[...] = jnp.where(lane64 < 64, wide[pl.ds(0, 64, stride=2), :], wide[pl.ds(1, 64, stride=2), :])

    low32 = lax.broadcasted_iota(jnp.int32, (32, 128), 1) < 64
    group = lax.shift_right_logical(lane64, 5).astype(I16)

    @pl.loop(0, 256 // UNROLL)
    def _(i):
        for u in range(UNROLL):
            p = i * UNROLL + u
            s = src_ref[p]
            e = tgt_ref[p]
            k = lax.shift_right_logical(s, 1) & 3
            start = lax.shift_right_logical(s, 3) * 128 + (s & 1) * 64
            value = jnp.where(group == k.astype(I16), source[aligned(start, 64), :], zero16)
            block = blocks[pl.ds(p * 33,32), :]
            rows = jnp.concatenate([jnp.where(low32, block, zero), jnp.where(low32, zero, block)], axis=0).astype(BF)
            total[aligned(e * 64, 64), :] += jnp.dot(
                rows, jnp.concatenate([value, value], axis=0), preferred_element_type=F32
            )

    lanes = lax.shift_right_logical(lax.broadcasted_iota(jnp.int32, (128, 128), 1), 5)
    odd = (lanes & 1) == 1
    up = lanes >= 2

    def join(a, b, mask, by):
        return jnp.where(mask, b, a) + pltpu.roll(jnp.where(mask, a, b), by, 1)

    @pl.loop(0, 16, unroll=True)
    def _(g):
        e = [total[aligned(g * 512 + j * 128, 128), :] for j in range(4)]
        both = join(join(e[0], e[1], odd, 32), join(e[2], e[3], odd, 32), up, 64).T
        for j in range(4):
            high, low = split2(both[j * TR : (j + 1) * TR])
            parts_ref[:, aligned(g * 512 + j * 128, 128)] = jnp.concatenate([high, low], axis=0)

    results = [
        pltpu.make_async_copy(a, b, sems.at[8 + i]) for i, (a, b) in enumerate(((ids_ref, ids_hbm), (parts_ref, parts_hbm)))
    ]
    for copy in results:
        copy.start()
    scatter_halo(ids_ref, parts_ref, acc)
    halves(acc, near_ref, far_ref)
    for copy in results:
        copy.wait()


def scatter_halo(ids_ref, parts_ref, acc):
    acc[...] = jnp.zeros_like(acc)

    @pl.loop(0, SLOTS // CHUNK, unroll=True)
    def _(k):
        add_scatter(
            acc, parts_ref[:, aligned(k * CHUNK, CHUNK)], ids_ref[aligned(k * TILES, TILES), :], TILES, OWN_BLOCKS, HALO_BLOCKS
        )


def upper_first():
    return lax.axis_index("c") == 0


def halves(acc, near_ref, far_ref):
    first, middle, last = (fold(acc, b) for b in range(HALO_BLOCKS))
    low = jnp.concatenate([first, middle[:, : F - L]], axis=1)
    high = jnp.concatenate([middle[:, F - L :], last], axis=1)
    upward = upper_first()
    near_ref[...] = jnp.where(upward, high, low)
    far_ref[...] = jnp.where(upward, low, high)


def arrived(near_ref, far_ref):
    upward = upper_first()
    near, far = near_ref[...], far_ref[...]
    return jnp.where(upward, near, far), jnp.where(upward, far, near)


def right_side_halo(tgt, src, conn, pair_blocks, source_values):
    return pl.pallas_call(
        rhs_kernel,
        out_shape=(shape((64, 128), jnp.int32), shape((2 * TR, SLOTS), BF), shape((TR, F)), shape((TR, F))),
        in_specs=hbm(5),
        out_specs=tuple(hbm(2) + vmem(2)),
        scratch_shapes=[
            pltpu.SMEM((256,), jnp.int32),
            pltpu.SMEM((256,), jnp.int32),
            pltpu.VMEM((64, 128), jnp.int32),
            pltpu.VMEM((256, 4096), BF),
            pltpu.VMEM((TR, SLOTS), BF),
            pltpu.VMEM((64, 128), jnp.int32),
            pltpu.VMEM((2 * TR, SLOTS), BF),
            pltpu.VMEM((8448, 128), F32),
            pltpu.VMEM((2048, 128), BF),
            pltpu.VMEM((8192, 128), F32),
            pltpu.VMEM((128, 128), jnp.int32),
            pltpu.VMEM((HALO_BLOCKS * 2 * TR, L), F32),
            pltpu.SemaphoreType.DMA((10,)),
        ],
        compiler_params=params(54),
        name="rhs",
    )(tgt, src, conn, pair_blocks, source_values)


def own_kernel(ids_ref, parts_ref, out_ref, acc):
    acc[...] = jnp.zeros_like(acc)

    @pl.loop(0, SLOTS // CHUNK, unroll=True)
    def _(k):
        add_scatter(acc, parts_ref[:, aligned(k * CHUNK, CHUNK)], ids_ref[aligned(k * TILES, TILES), :], TILES, 0, OWN_BLOCKS)

    for b in range(OWN_BLOCKS):
        out_ref[:, b * L : (b + 1) * L] = fold(acc, b)


def scatter_own(ids, parts):
    return pl.pallas_call(
        own_kernel,
        out_shape=shape((TR, OWN_BLOCKS * L)),
        in_specs=vmem(2),
        out_specs=vmem(1)[0],
        scratch_shapes=[pltpu.VMEM((OWN_BLOCKS * 2 * TR, L), F32)],
        compiler_params=params(),
        cost_estimate=pl.CostEstimate(flops=2 * 448 * 512 * 8192, bytes_accessed=2**21, transcendentals=0),
        name="own",
    )(ids, parts)


def settle(own_ref, near_ref, far_ref, highs_ref, lows_ref, acc):
    rows = [highs_ref[:, j * 128 : (j + 1) * 128] for j in range(6)] + [lows_ref[:, j * 128 : (j + 1) * 128] for j in range(6)]
    hot = jnp.concatenate([one_hot(r & (L - 1)) for r in rows], axis=1)
    blocks = [lax.shift_right_logical(r, 9) for r in rows]
    high, low = split2(jnp.concatenate(arrived(near_ref, far_ref), axis=1))
    parts = jnp.concatenate([high, low], axis=0)
    acc[...] = lax.dot_general(masked(parts, blocks, 0, OWN_BLOCKS), hot, NT, preferred_element_type=F32)
    whole = [own_ref[:, b * L : (b + 1) * L] + fold(acc, b) for b in range(OWN_BLOCKS)]
    return whole, hot, blocks


def settle_kernel(own_ref, near_ref, far_ref, highs_ref, lows_ref, out_ref, near_out, far_out, table_ref, acc):
    whole, hot, blocks = settle(own_ref, near_ref, far_ref, highs_ref, lows_ref, acc)
    for b, value in enumerate(whole):
        end = min(NODE_DEV, (b + 1) * L)
        out_ref[:, b * L : end] = value[:, : end - b * L]
        high, low = split2(value)
        table_ref[b * TR : (b + 1) * TR, :] = jnp.concatenate([high, low], axis=1)
    rows = jnp.dot(table_ref[...], jnp.concatenate([hot, hot], axis=0), preferred_element_type=F32)
    zeros = [jnp.zeros((TR, 128), F32)] * 12
    values = picked(rows, blocks, 0, OWN_BLOCKS, zeros)
    upward = upper_first()
    for j in range(6):
        near_out[:, j * 128 : (j + 1) * 128] = jnp.where(upward, values[j], values[6 + j])
        far_out[:, j * 128 : (j + 1) * 128] = jnp.where(upward, values[6 + j], values[j])


def settle_right(own, near, far, highs, lows):
    return pl.pallas_call(
        settle_kernel,
        out_shape=(
            shape((TR, NODE_DEV)),
            shape((TR, F)),
            shape((TR, F)),
            shape((OWN_BLOCKS * TR, 2 * L), BF),
        ),
        in_specs=vmem(5),
        out_specs=tuple(vmem(4)),
        scratch_shapes=[pltpu.VMEM((OWN_BLOCKS * 2 * TR, L), F32)],
        compiler_params=params(),
        name="settle",
    )(own, near, far, highs, lows)


def gather_kernel(ids_ref, table_ref, jac_ref, out_ref, scale_ref, wide):
    wide[...] = jnp.broadcast_to(jac_ref[...], (128, 128)).T
    lane64 = lax.broadcasted_iota(jnp.int32, (64, 128), 1)
    scale_ref[...] = jnp.where(lane64 < 64, wide[pl.ds(0, 64, stride=2), :], wide[pl.ds(1, 64, stride=2), :])

    @pl.loop(0, SLOTS // CHUNK, unroll=True)
    def _(k):
        hot, blocks = tiles_of(ids_ref[aligned(k * TILES, TILES), :], TILES)
        rows = jnp.dot(table_ref[...], jnp.concatenate([hot, hot], axis=0), preferred_element_type=F32)
        values = picked(rows, blocks, 0, OWN_BLOCKS, [jnp.zeros((TR, 128), F32)] * TILES)
        out_ref[:, aligned(k * CHUNK, CHUNK)] = jnp.concatenate(values, axis=1)


def gather_own(ids, table, jac):
    return pl.pallas_call(
        gather_kernel,
        out_shape=(shape((TR, SLOTS)), shape((64, 128))),
        in_specs=vmem(3),
        out_specs=tuple(vmem(2)),
        scratch_shapes=[pltpu.VMEM((128, 128), F32)],
        compiler_params=params(),
        cost_estimate=pl.CostEstimate(flops=2 * 448 * 512 * 8192, bytes_accessed=2**21, transcendentals=0),
        name="gather",
    )(ids, table, jac)


def mass_kernel(ids_ref, start_ref, near_ref, far_ref, scale_ref, mass_ref, parts_ref, near_out, far_out, table, acc):
    above, below = arrived(near_ref, far_ref)
    both = jnp.concatenate([below, above], axis=1)
    for b in range(HALO_BLOCKS):
        high, low = split2(both[:, b * L : (b + 1) * L])
        table[b * 2 * TR : (b + 1) * 2 * TR, :] = jnp.concatenate([high, low], axis=0)
    acc[...] = jnp.zeros_like(acc)

    @pl.loop(0, SLOTS // CHUNK, unroll=True)
    def _(k):
        hot, blocks = tiles_of(ids_ref[aligned(k * TILES, TILES), :], TILES)
        rows = jnp.dot(table[...], hot, preferred_element_type=F32)
        zeros = [jnp.zeros((2 * TR, 128), F32)] * TILES
        found = picked(rows, blocks, OWN_BLOCKS, HALO_BLOCKS, zeros)
        values = [
            start_ref[:, aligned(k * CHUNK + j * 128, 128)] + found[j][:TR] + found[j][TR:] for j in range(TILES)
        ]
        split = [split2(jnp.concatenate(values[2 * j : 2 * j + 2], axis=1)) for j in range(TILES // 2)]
        highs = jnp.concatenate([s[0] for s in split], axis=0)
        lows = jnp.concatenate([s[1] for s in split], axis=0)
        image = (
            jnp.dot(highs, mass_ref[:, :256], preferred_element_type=F32)
            + jnp.dot(lows, mass_ref[:, :256], preferred_element_type=F32)
            + jnp.dot(highs, mass_ref[:, 256:], preferred_element_type=F32)
        )
        tiles = []
        scales = scale_ref[aligned(k * TILES, TILES), :]
        for j in range(TILES):
            tile = image[(j // 2) * TR : (j // 2 + 1) * TR, (j % 2) * 128 : (j % 2 + 1) * 128]
            high, low = split2(tile * scales[j : j + 1])
            tiles.append(jnp.concatenate([high, low], axis=0))
        parts = jnp.concatenate(tiles, axis=1)
        parts_ref[:, aligned(k * CHUNK, CHUNK)] = parts
        acc[...] += lax.dot_general(
            masked(parts, blocks, OWN_BLOCKS, HALO_BLOCKS), hot, NT, preferred_element_type=F32
        )

    halves(acc, near_out, far_out)


def mass_halo(ids, start, near, far, scale, mass):
    return pl.pallas_call(
        mass_kernel,
        out_shape=(shape((2 * TR, SLOTS), BF), shape((TR, F)), shape((TR, F))),
        in_specs=vmem(6),
        out_specs=tuple(vmem(3)),
        scratch_shapes=[
            pltpu.VMEM((HALO_BLOCKS * 2 * TR, L), BF),
            pltpu.VMEM((HALO_BLOCKS * 2 * TR, L), F32),
        ],
        compiler_params=params(),
        name="mass",
    )(ids, start, near, far, scale, mass)


def places():
    return tuple(lax.broadcasted_iota(jnp.int32, (TR, TR), i) for i in range(2))


def lay_flat(square):
    return jnp.concatenate([square[8 * i : 8 * i + 8] for i in range(4)], axis=1)


def lay_square(flat):
    return jnp.concatenate([flat[:, 32 * i : 32 * i + 32] for i in range(4)], axis=0)


def gram_kernel(own_ref, near_ref, far_ref, highs_ref, lows_ref, right_ref, out_ref, gram_ref, acc):
    whole, _, _ = settle(own_ref, near_ref, far_ref, highs_ref, lows_ref, acc)
    for b, value in enumerate(whole):
        end = min(NODE_DEV, (b + 1) * L)
        out_ref[:, b * L : end] = value[:, : end - b * L]
    right = split2(right_ref[...])
    image = split2(out_ref[...])
    stack = jnp.concatenate([right[0], image[0], right[1], image[1]], axis=0)
    full = lax.dot_general(stack, stack, NT, preferred_element_type=F32)
    full = full[:64] + full[64:]
    full = full[:, :64] + full[:, 64:]
    cross = full[:TR, TR:]
    cross = 0.5 * (cross + full[TR:, :TR])
    rhs, images = full[:TR, :TR], full[TR:, TR:]
    row, col = places()
    diagonal = jnp.sum(jnp.where(row == col, images, 0.0), axis=0, keepdims=True)
    first = jnp.where(row >= col, rhs, images)
    second = jnp.where(row == 0, diagonal, images[:1, :1])
    gram_ref[0:8, :] = lay_flat(first)
    gram_ref[8:16, :] = lay_flat(jnp.where(row >= col, cross, second))


def grams(own, near, far, highs, lows, right):
    return pl.pallas_call(
        gram_kernel,
        out_shape=(shape((TR, NODE_DEV)), shape((16, 128))),
        in_specs=vmem(6),
        out_specs=tuple(vmem(2)),
        scratch_shapes=[pltpu.VMEM((OWN_BLOCKS * 2 * TR, L), F32)],
        compiler_params=params(),
        name="grams",
    )(own, near, far, highs, lows, right)


def hdot(a, b, dims=(((1,), (0,)), ((), ()))):
    return lax.dot_general(a, b, dims, precision=lax.Precision.HIGHEST, preferred_element_type=F32)


def eliminate(work, above):
    groups = TR // 8
    row = lax.broadcasted_iota(jnp.int32, (8, 128), 0)
    work = [work[8 * g : 8 * g + 8] for g in range(groups)]
    scale = [jnp.zeros((8, 128), F32)] * groups
    for panel in range(groups):
        columns = {
            k: [jnp.broadcast_to(work[g][:, k : k + 1], (8, 128)) for g in range(groups)]
            for k in range(8 * panel, 8 * panel + 8)
        }
        for k in range(8 * panel, 8 * panel + 8):
            g0, r = divmod(k, 8)
            column = columns[k]
            pivot = column[g0][r : r + 1]
            inverse = 1.0 / pivot
            if not above:
                scale[g0] = jnp.where(row == r, jnp.broadcast_to(pivot, (8, 128)), scale[g0])

            def update(target):
                line = jnp.broadcast_to(target[g0][r : r + 1] * inverse, (8, 128))
                out = []
                for g in range(groups):
                    if g < g0 and not above:
                        out.append(target[g])
                    elif g == g0:
                        less = target[g] - column[g] * line
                        if above:
                            out.append(jnp.where(row == r, line, less))
                        else:
                            out.append(jnp.where(row > r, less, target[g]))
                    else:
                        out.append(target[g] - column[g] * line)
                return out

            work = update(work)
            for j in range(k + 1, 8 * panel + 8):
                columns[j] = update(columns[j])
    if not above:
        work = [w * lax.rsqrt(s) for w, s in zip(work, scale)]
    return jnp.concatenate(work, axis=0)


def final_kernel(gram_ref, right_ref, image_ref, sol_ref, res_ref, new_ref):
    total = gram_ref[0]
    for i in range(1, gram_ref.shape[0]):
        total = total + gram_ref[i]
    first = lay_square(total[:8])
    second = lay_square(total[8:])
    first_t = first.T
    second_t = second.T
    row, col = places()
    rhs = jnp.where(row >= col, first, first_t)
    cross = jnp.where(row >= col, second, second_t)
    diagonal = jnp.where(col == 0, second[1:2, 2:3], second[:1, :])
    images = jnp.where(row < col, first, jnp.where(row == col, diagonal, first_t))
    zero = jnp.zeros((TR, TR), F32)
    eye = jnp.where(row == col, 1.0, 0.0)

    weights_t = eliminate(jnp.concatenate([cross, rhs, zero, zero], axis=1), True)[:, TR : 2 * TR]
    weights = weights_t.T
    both = hdot(weights, jnp.concatenate([cross, images], axis=1))
    gram = rhs - 2.0 * both[:, :TR] + hdot(both[:, TR:], weights_t)
    work = eliminate(jnp.concatenate([gram, eye, weights, zero], axis=1), False)
    inverse = work[:, TR : 2 * TR]
    mixed = work[:, 2 * TR : 3 * TR]
    coeffs = jnp.concatenate(
        [
            jnp.concatenate([weights, zero], axis=1),
            jnp.concatenate([zero, -weights], axis=1),
            jnp.concatenate([inverse, -mixed], axis=1),
        ],
        axis=0,
    )
    high, low = split2(coeffs)
    right = right_ref[...]
    rh, rl = split2(right)
    ih, il = split2(image_ref[...])
    highs = jnp.concatenate([rh, ih], axis=0)
    lows = jnp.concatenate([rl, il], axis=0)
    out = (
        jnp.dot(high, highs, preferred_element_type=F32)
        + jnp.dot(high, lows, preferred_element_type=F32)
        + jnp.dot(low, highs, preferred_element_type=F32)
    )
    sol_ref[...] = out[:TR]
    res_ref[...] = right + out[TR : 2 * TR]
    new_ref[...] = out[2 * TR :]


def finish(gram, right, image):
    return pl.pallas_call(
        final_kernel,
        out_shape=(shape((TR, NODE_DEV)),) * 3,
        in_specs=vmem(3),
        out_specs=tuple(vmem(3)),
        compiler_params=params(),
        name="finish",
    )(gram, right, image)


def swapped(near, far):
    outer = [(i, j) for k in range(1, 511, 2) for i, j in ((k, k + 1), (k + 1, k))]
    far = lax.ppermute(far, AXES, outer)
    near = lax.ppermute(near, AXES, [(i, i ^ 1) for i in range(512)])
    return near, far


def exchanged(value, axes):
    count = int(np.prod([SIZES[a] for a in axes]))
    copies = lax.optimization_barrier(jnp.broadcast_to(value[None], (count,) + value.shape))
    return lax.all_to_all(copies, axes, 0, 0)


def per_device(connectivity, send_down, send_up, jacobian, pair_blocks, pair_target, pair_source, source_values):
    lows = send_down
    highs = send_up
    mass = jnp.asarray(mass_tiles())
    ids, parts, near, far = right_side_halo(pair_target, pair_source, connectivity.T, pair_blocks, source_values)
    near, far = swapped(near, far)
    own = scatter_own(ids, parts)
    right, near, far, table = settle_right(own, near, far, highs, lows)
    near, far = swapped(near, far)
    start, scale = gather_own(ids, table, jacobian[None, :])
    parts, near, far = mass_halo(ids, start, near, far, scale, mass)
    near, far = swapped(near, far)
    own = scatter_own(ids, parts)
    image, gram = grams(own, near, far, highs, lows, right)
    gram = exchanged(gram, ("x", "y")).sum(0)
    gram = exchanged(gram, ("z", "c"))
    return finish(gram, right, image)


def solution(mesh):
    mesh = Mesh(mesh.devices.reshape(4, 8, 8, 2), AXES)
    return jax.shard_map(
        per_device,
        mesh=mesh,
        in_specs=(
            P(AXES, None),
            P(AXES, None),
            P(AXES, None),
            P(AXES),
            P(AXES, None),
            P(AXES),
            P(AXES),
            P(None, AXES),
        ),
        out_specs=(P(None, AXES), P(None, AXES), P(None, AXES)),
        check_vma=False,
    )
```

```python
import jax
import jax.numpy as jnp
import numpy as np
from jax import lax
from jax.experimental import pallas as pl
from jax.experimental.pallas import tpu as pltpu
from jax.sharding import Mesh
from jax.sharding import PartitionSpec as P

TR = 32
NODE_DEV = 3456
F = 768
SLOTS = 8192
L = 512
OWN_BLOCKS = 7
HALO = 256
HALO_FIRST = OWN_BLOCKS * L // HALO
HALO_BLOCKS = 6
PAD = OWN_BLOCKS * L - NODE_DEV
BF = jnp.bfloat16
F32 = jnp.float32
I16 = jnp.int16
NT = (((1,), (1,)), ((), ()))
AXES = ("x", "z", "y", "c")
SIZES = {"x": 4, "z": 8, "y": 8, "c": 2}

line_mass = (
    np.array(
        [
            [128.0, 99.0, -36.0, 19.0],
            [99.0, 648.0, -81.0, -36.0],
            [-36.0, -81.0, 648.0, 99.0],
            [19.0, -36.0, 99.0, 128.0],
        ]
    )
    / 504.0
)
mass_table = np.kron(np.kron(line_mass, line_mass), line_mass)


def mass_tiles():
    order = np.arange(64).reshape(32, 2).T.reshape(-1)
    block = mass_table[np.ix_(order, order)].astype(np.float32)
    whole = np.kron(np.eye(4, dtype=np.float32), block)
    high = whole.astype(jnp.bfloat16)
    low = (whole - high.astype(np.float32)).astype(jnp.bfloat16)
    return np.concatenate([high, low], axis=1)


def params(mebibytes=24):
    return pltpu.CompilerParams(vmem_limit_bytes=mebibytes * 2**20)


def vmem(count):
    return [pl.BlockSpec(memory_space=pltpu.VMEM)] * count


def hbm(count):
    return [pl.BlockSpec(memory_space=pltpu.MemorySpace.HBM)] * count


def shape(dims, kind=F32):
    return jax.ShapeDtypeStruct(dims, kind)


def aligned(start, size):
    return pl.ds(pl.multiple_of(start, size), size)


def split2(value):
    high = value.astype(BF)
    low = (value - high.astype(F32)).astype(BF)
    return high, low


def one_hot(row, size=L):
    spread = jnp.broadcast_to(row.astype(I16), (size, 128))
    index = lax.broadcasted_iota(I16, (size, 128), 0)
    return jnp.where(spread == index, jnp.ones((), BF), jnp.zeros((), BF))


def tiles_of(ids, count, size=L):
    blocks = lax.shift_right_logical(ids, size.bit_length() - 1)
    places = ids & (size - 1)
    hot = jnp.concatenate([one_hot(places[j : j + 1], size) for j in range(count)], axis=1)
    return hot, [blocks[j : j + 1] for j in range(count)]


def masked(parts, blocks, first, number):
    out = []
    for j, row in enumerate(blocks):
        here = jnp.broadcast_to(row.astype(I16), (2 * TR, 128))
        tile = parts[:, j * 128 : (j + 1) * 128]
        out.append(
            jnp.concatenate(
                [jnp.where(here == first + b, tile, jnp.zeros((), BF)) for b in range(number)], axis=0
            )
        )
    return jnp.concatenate(out, axis=1)


def picked(rows, blocks, first, number, start):
    out = []
    for j, row in enumerate(blocks):
        tile = start[j]
        height = tile.shape[0]
        here = jnp.broadcast_to(row, (height, 128))
        for b in range(number):
            tile = jnp.where(here == first + b, rows[b * height : (b + 1) * height, j * 128 : (j + 1) * 128], tile)
        out.append(tile)
    return out


def add_scatter(acc, parts, ids, count, first, number, size=L):
    hot, blocks = tiles_of(ids, count, size)
    acc[...] += lax.dot_general(
        masked(parts, blocks, first, number), hot, NT, preferred_element_type=F32
    )


def fold(acc, b):
    return acc[b * 2 * TR : b * 2 * TR + TR] + acc[b * 2 * TR + TR : (b + 1) * 2 * TR]


CHUNK = 2048
TILES = CHUNK // 128
UNROLL = 128


def rhs_kernel(
    tgt_hbm,
    src_hbm,
    conn_hbm,
    pb_hbm,
    sv_hbm,
    ids_hbm,
    parts_hbm,
    near_ref,
    far_ref,
    tgt_ref,
    src_ref,
    conn_ref,
    pb_ref,
    sv_ref,
    ids_ref,
    parts_ref,
    blocks,
    source,
    total,
    wide,
    acc,
    sems,
):
    zero = jnp.zeros((), F32)
    zero16 = jnp.zeros((), BF)
    small = [
        pltpu.make_async_copy(a, b, sems.at[i])
        for i, (a, b) in enumerate(((sv_hbm, sv_ref), (conn_hbm, conn_ref), (tgt_hbm, tgt_ref), (src_hbm, src_ref)))
    ]
    large = [
        pltpu.make_async_copy(pb_hbm.at[pl.ds(64 * i, 64), :], pb_ref.at[pl.ds(64 * i, 64), :], sems.at[4 + i]) for i in range(4)
    ]
    for copy in small + large:
        copy.start()
    total[...] = jnp.zeros_like(total)
    small[0].wait()
    for g in range(16):
        stack = jnp.concatenate([sv_ref[:, (4 * g + k) * 128 : (4 * g + k + 1) * 128] for k in range(4)], axis=0)
        source[g * 128 : (g + 1) * 128, :] = stack.astype(F32).T.astype(BF)
    for copy in small[1:]:
        copy.wait()
    for i in range(4):
        large[i].wait()

        @pl.loop(4 * i, 4 * i + 4)
        def _(g):
            for c in range(32):
                rows = pb_ref[aligned(g * 16, 16), c * 128 : (c + 1) * 128].astype(F32)
                blocks[pl.ds(g * 528 + c, 16, stride=33), :] = rows

    conn = conn_ref[...].astype(F32).T.astype(jnp.int32)
    row = lax.broadcasted_iota(jnp.int32, (64, 64), 0)
    col = lax.broadcasted_iota(jnp.int32, (64, 64), 1)
    swap = jnp.where(row == 2 * (col & 31) + lax.shift_right_logical(col, 5), 1.0, 0.0).astype(BF)
    upper = lax.shift_right_logical(conn, 7).astype(F32).astype(BF)
    lower = (conn & 127).astype(F32).astype(BF)
    ids = jnp.dot(upper, swap, preferred_element_type=F32) * 128.0 + jnp.dot(lower, swap, preferred_element_type=F32)
    ids = ids.astype(jnp.int32)
    ids = jnp.where(ids >= NODE_DEV, ids + PAD, ids)
    wide[...] = jnp.concatenate([ids, ids], axis=1)
    lane64 = lax.broadcasted_iota(jnp.int32, (64, 128), 1)
    ids_ref[...] = jnp.where(lane64 < 64, wide[pl.ds(0, 64, stride=2), :], wide[pl.ds(1, 64, stride=2), :])

    low32 = lax.broadcasted_iota(jnp.int32, (32, 128), 1) < 64
    group = lax.shift_right_logical(lane64, 5).astype(I16)

    @pl.loop(0, 256 // UNROLL)
    def _(i):
        for u in range(UNROLL):
            p = i * UNROLL + u
            s = src_ref[p]
            e = tgt_ref[p]
            k = lax.shift_right_logical(s, 1) & 3
            start = lax.shift_right_logical(s, 3) * 128 + (s & 1) * 64
            value = jnp.where(group == k.astype(I16), source[aligned(start, 64), :], zero16)
            block = blocks[pl.ds(p * 33,32), :]
            rows = jnp.concatenate([jnp.where(low32, block, zero), jnp.where(low32, zero, block)], axis=0).astype(BF)
            total[aligned(e * 64, 64), :] += jnp.dot(
                rows, jnp.concatenate([value, value], axis=0), preferred_element_type=F32
            )

    lanes = lax.shift_right_logical(lax.broadcasted_iota(jnp.int32, (128, 128), 1), 5)
    odd = (lanes & 1) == 1
    up = lanes >= 2

    def join(a, b, mask, by):
        return jnp.where(mask, b, a) + pltpu.roll(jnp.where(mask, a, b), by, 1)

    @pl.loop(0, 16, unroll=True)
    def _(g):
        e = [total[aligned(g * 512 + j * 128, 128), :] for j in range(4)]
        both = join(join(e[0], e[1], odd, 32), join(e[2], e[3], odd, 32), up, 64).T
        for j in range(4):
            high, low = split2(both[j * TR : (j + 1) * TR])
            parts_ref[:, aligned(g * 512 + j * 128, 128)] = jnp.concatenate([high, low, id_rows(ids_ref[pl.ds(4 * g + j, 1), :])], axis=0)

    results = [
        pltpu.make_async_copy(a, b, sems.at[8 + i]) for i, (a, b) in enumerate(((ids_ref, ids_hbm), (parts_ref, parts_hbm)))
    ]
    for copy in results:
        copy.start()
    scatter_halo(ids_ref, parts_ref, acc)
    halves(acc, near_ref, far_ref)
    for copy in results:
        copy.wait()


def id_rows(ids):
    row = lax.broadcasted_iota(jnp.int32, (16, 128), 0)
    ids = jnp.broadcast_to(ids, (16, 128))
    block = lax.shift_right_logical(ids, 9)
    half = lax.shift_right_logical(ids, 8) & 1
    return jnp.where(row == 0, block, jnp.where(row == 1, half, ids & 255)).astype(F32).astype(BF)


def rows_to_ids(rows):
    rows = rows.astype(F32)
    return (rows[0:1] * 512.0 + rows[1:2] * 256.0 + rows[2:3]).astype(jnp.int32)


def own_first_kernel(parts_hbm, out_ref, parts_ref, acc, sems):
    copies = [
        pltpu.make_async_copy(
            parts_hbm.at[:, pl.ds(k * CHUNK, CHUNK)], parts_ref.at[:, pl.ds(k * CHUNK, CHUNK)], sems.at[k]
        )
        for k in range(SLOTS // CHUNK)
    ]
    for copy in copies:
        copy.start()
    acc[...] = jnp.zeros_like(acc)
    for k, copy in enumerate(copies):
        copy.wait()
        ids = jnp.concatenate(
            [rows_to_ids(parts_ref[2 * TR :, k * CHUNK + j * 128 : k * CHUNK + (j + 1) * 128]) for j in range(TILES)], axis=0
        )
        add_scatter(acc, parts_ref[: 2 * TR, k * CHUNK : (k + 1) * CHUNK], ids, TILES, 0, OWN_BLOCKS)
    for b in range(OWN_BLOCKS):
        out_ref[:, b * L : (b + 1) * L] = fold(acc, b)


def scatter_own_first(parts):
    return pl.pallas_call(
        own_first_kernel,
        out_shape=shape((TR, OWN_BLOCKS * L)),
        in_specs=hbm(1),
        out_specs=vmem(1)[0],
        scratch_shapes=[
            pltpu.VMEM((2 * TR + 16, SLOTS), BF),
            pltpu.VMEM((OWN_BLOCKS * 2 * TR, L), F32),
            pltpu.SemaphoreType.DMA((SLOTS // CHUNK,)),
        ],
        compiler_params=pltpu.CompilerParams(vmem_limit_bytes=54784 * 2**10),
        cost_estimate=pl.CostEstimate(flops=2 * 448 * 512 * 8192, bytes_accessed=2**21, transcendentals=0),
        name="own_first",
    )(parts)


def scatter_halo(ids_ref, parts_ref, acc):
    acc[...] = jnp.zeros_like(acc)

    @pl.loop(0, SLOTS // CHUNK, unroll=True)
    def _(k):
        add_scatter(
            acc,
            parts_ref[: 2 * TR, aligned(k * CHUNK, CHUNK)],
            ids_ref[aligned(k * TILES, TILES), :],
            TILES,
            HALO_FIRST,
            HALO_BLOCKS,
            HALO,
        )


def upper_first():
    return lax.axis_index("c") == 0


def halves(acc, near_ref, far_ref):
    half = HALO_BLOCKS // 2
    low, high = (jnp.concatenate([fold(acc, b) for b in range(i, i + half)], axis=1) for i in (0, half))
    upward = upper_first()
    near_ref[...] = jnp.where(upward, high, low)
    far_ref[...] = jnp.where(upward, low, high)


def arrived(near_ref, far_ref):
    upward = upper_first()
    near, far = near_ref[...], far_ref[...]
    return jnp.where(upward, near, far), jnp.where(upward, far, near)


def right_side_halo(tgt, src, conn, pair_blocks, source_values):
    return pl.pallas_call(
        rhs_kernel,
        out_shape=(shape((64, 128), jnp.int32), shape((2 * TR + 16, SLOTS), BF), shape((TR, F)), shape((TR, F))),
        in_specs=hbm(5),
        out_specs=tuple(hbm(2) + vmem(2)),
        scratch_shapes=[
            pltpu.SMEM((256,), jnp.int32),
            pltpu.SMEM((256,), jnp.int32),
            pltpu.VMEM((64, 128), jnp.int32),
            pltpu.VMEM((256, 4096), BF),
            pltpu.VMEM((TR, SLOTS), BF),
            pltpu.VMEM((64, 128), jnp.int32),
            pltpu.VMEM((2 * TR + 16, SLOTS), BF),
            pltpu.VMEM((8448, 128), F32),
            pltpu.VMEM((2048, 128), BF),
            pltpu.VMEM((8192, 128), F32),
            pltpu.VMEM((128, 128), jnp.int32),
            pltpu.VMEM((HALO_BLOCKS * 2 * TR, HALO), F32),
            pltpu.SemaphoreType.DMA((10,)),
        ],
        compiler_params=params(54),
        name="rhs",
    )(tgt, src, conn, pair_blocks, source_values)


def own_kernel(ids_ref, parts_ref, out_ref, acc):
    acc[...] = jnp.zeros_like(acc)

    @pl.loop(0, SLOTS // CHUNK, unroll=True)
    def _(k):
        add_scatter(acc, parts_ref[:, aligned(k * CHUNK, CHUNK)], ids_ref[aligned(k * TILES, TILES), :], TILES, 0, OWN_BLOCKS)

    for b in range(OWN_BLOCKS):
        out_ref[:, b * L : (b + 1) * L] = fold(acc, b)


def scatter_own(ids, parts):
    return pl.pallas_call(
        own_kernel,
        out_shape=shape((TR, OWN_BLOCKS * L)),
        in_specs=vmem(2),
        out_specs=vmem(1)[0],
        scratch_shapes=[pltpu.VMEM((OWN_BLOCKS * 2 * TR, L), F32)],
        compiler_params=params(),
        cost_estimate=pl.CostEstimate(flops=2 * 448 * 512 * 8192, bytes_accessed=2**21, transcendentals=0),
        name="own",
    )(ids, parts)


def settle(own_ref, near_ref, far_ref, highs_ref, lows_ref, acc):
    rows = [highs_ref[:, j * 128 : (j + 1) * 128] for j in range(6)] + [lows_ref[:, j * 128 : (j + 1) * 128] for j in range(6)]
    hot = jnp.concatenate([one_hot(r & (L - 1)) for r in rows], axis=1)
    blocks = [lax.shift_right_logical(r, L.bit_length() - 1) for r in rows]
    high, low = split2(jnp.concatenate(arrived(near_ref, far_ref), axis=1))
    parts = jnp.concatenate([high, low], axis=0)
    acc[...] = lax.dot_general(masked(parts, blocks, 0, OWN_BLOCKS), hot, NT, preferred_element_type=F32)
    whole = [own_ref[:, b * L : (b + 1) * L] + fold(acc, b) for b in range(OWN_BLOCKS)]
    return whole, hot, blocks


def settle_kernel(own_ref, near_ref, far_ref, highs_ref, lows_ref, out_ref, near_out, far_out, table_ref, acc):
    whole, hot, blocks = settle(own_ref, near_ref, far_ref, highs_ref, lows_ref, acc)
    for b, value in enumerate(whole):
        end = min(NODE_DEV, (b + 1) * L)
        out_ref[:, b * L : end] = value[:, : end - b * L]
        high, low = split2(value)
        table_ref[b * TR : (b + 1) * TR, :] = jnp.concatenate([high, low], axis=1)
    rows = jnp.dot(table_ref[...], jnp.concatenate([hot, hot], axis=0), preferred_element_type=F32)
    zeros = [jnp.zeros((TR, 128), F32)] * 12
    values = picked(rows, blocks, 0, OWN_BLOCKS, zeros)
    upward = upper_first()
    for j in range(6):
        near_out[:, j * 128 : (j + 1) * 128] = jnp.where(upward, values[j], values[6 + j])
        far_out[:, j * 128 : (j + 1) * 128] = jnp.where(upward, values[6 + j], values[j])


def settle_right(own, near, far, highs, lows):
    return pl.pallas_call(
        settle_kernel,
        out_shape=(
            shape((TR, NODE_DEV)),
            shape((TR, F)),
            shape((TR, F)),
            shape((OWN_BLOCKS * TR, 2 * L), BF),
        ),
        in_specs=vmem(5),
        out_specs=tuple(vmem(4)),
        scratch_shapes=[pltpu.VMEM((OWN_BLOCKS * 2 * TR, L), F32)],
        compiler_params=params(),
        name="settle",
    )(own, near, far, highs, lows)


def gather_kernel(ids_ref, table_ref, jac_ref, out_ref, scale_ref, wide):
    wide[...] = jnp.broadcast_to(jac_ref[...], (128, 128)).T
    lane64 = lax.broadcasted_iota(jnp.int32, (64, 128), 1)
    scale_ref[...] = jnp.where(lane64 < 64, wide[pl.ds(0, 64, stride=2), :], wide[pl.ds(1, 64, stride=2), :])

    @pl.loop(0, SLOTS // CHUNK, unroll=True)
    def _(k):
        hot, blocks = tiles_of(ids_ref[aligned(k * TILES, TILES), :], TILES)
        rows = jnp.dot(table_ref[...], jnp.concatenate([hot, hot], axis=0), preferred_element_type=F32)
        values = picked(rows, blocks, 0, OWN_BLOCKS, [jnp.zeros((TR, 128), F32)] * TILES)
        out_ref[:, aligned(k * CHUNK, CHUNK)] = jnp.concatenate(values, axis=1)


def gather_own(ids, table, jac):
    return pl.pallas_call(
        gather_kernel,
        out_shape=(shape((TR, SLOTS)), shape((64, 128))),
        in_specs=vmem(3),
        out_specs=tuple(vmem(2)),
        scratch_shapes=[pltpu.VMEM((128, 128), F32)],
        compiler_params=params(),
        cost_estimate=pl.CostEstimate(flops=2 * 448 * 512 * 8192, bytes_accessed=2**21, transcendentals=0),
        name="gather",
    )(ids, table, jac)


def mass_kernel(ids_ref, start_ref, near_ref, far_ref, scale_ref, mass_ref, parts_ref, near_out, far_out, table, acc):
    above, below = arrived(near_ref, far_ref)
    both = jnp.concatenate([below, above], axis=1)
    for b in range(HALO_BLOCKS):
        high, low = split2(both[:, b * HALO : (b + 1) * HALO])
        table[b * 2 * TR : (b + 1) * 2 * TR, :] = jnp.concatenate([high, low], axis=0)
    acc[...] = jnp.zeros_like(acc)

    @pl.loop(0, SLOTS // CHUNK, unroll=True)
    def _(k):
        hot, blocks = tiles_of(ids_ref[aligned(k * TILES, TILES), :], TILES, HALO)
        rows = jnp.dot(table[...], hot, preferred_element_type=F32)
        zeros = [jnp.zeros((2 * TR, 128), F32)] * TILES
        found = picked(rows, blocks, HALO_FIRST, HALO_BLOCKS, zeros)
        values = [
            start_ref[:, aligned(k * CHUNK + j * 128, 128)] + found[j][:TR] + found[j][TR:] for j in range(TILES)
        ]
        split = [split2(jnp.concatenate(values[2 * j : 2 * j + 2], axis=1)) for j in range(TILES // 2)]
        highs = jnp.concatenate([s[0] for s in split], axis=0)
        lows = jnp.concatenate([s[1] for s in split], axis=0)
        image = (
            jnp.dot(highs, mass_ref[:, :256], preferred_element_type=F32)
            + jnp.dot(lows, mass_ref[:, :256], preferred_element_type=F32)
            + jnp.dot(highs, mass_ref[:, 256:], preferred_element_type=F32)
        )
        tiles = []
        scales = scale_ref[aligned(k * TILES, TILES), :]
        for j in range(TILES):
            tile = image[(j // 2) * TR : (j // 2 + 1) * TR, (j % 2) * 128 : (j % 2 + 1) * 128]
            high, low = split2(tile * scales[j : j + 1])
            tiles.append(jnp.concatenate([high, low], axis=0))
        parts = jnp.concatenate(tiles, axis=1)
        parts_ref[:, aligned(k * CHUNK, CHUNK)] = parts
        acc[...] += lax.dot_general(
            masked(parts, blocks, HALO_FIRST, HALO_BLOCKS), hot, NT, preferred_element_type=F32
        )

    halves(acc, near_out, far_out)


def mass_halo(ids, start, near, far, scale, mass):
    return pl.pallas_call(
        mass_kernel,
        out_shape=(shape((2 * TR, SLOTS), BF), shape((TR, F)), shape((TR, F))),
        in_specs=vmem(6),
        out_specs=tuple(vmem(3)),
        scratch_shapes=[
            pltpu.VMEM((HALO_BLOCKS * 2 * TR, HALO), BF),
            pltpu.VMEM((HALO_BLOCKS * 2 * TR, HALO), F32),
        ],
        compiler_params=params(),
        name="mass",
    )(ids, start, near, far, scale, mass)


def places():
    return tuple(lax.broadcasted_iota(jnp.int32, (TR, TR), i) for i in range(2))


def lay_flat(square):
    return jnp.concatenate([square[8 * i : 8 * i + 8] for i in range(4)], axis=1)


def lay_square(flat):
    return jnp.concatenate([flat[:, 32 * i : 32 * i + 32] for i in range(4)], axis=0)


def gram_kernel(own_ref, near_ref, far_ref, highs_ref, lows_ref, right_ref, out_ref, gram_ref, acc):
    whole, _, _ = settle(own_ref, near_ref, far_ref, highs_ref, lows_ref, acc)
    for b, value in enumerate(whole):
        end = min(NODE_DEV, (b + 1) * L)
        out_ref[:, b * L : end] = value[:, : end - b * L]
    right = split2(right_ref[...])
    image = split2(out_ref[...])
    stack = jnp.concatenate([right[0], image[0], right[1], image[1]], axis=0)
    full = lax.dot_general(stack, stack, NT, preferred_element_type=F32)
    full = full[:64] + full[64:]
    full = full[:, :64] + full[:, 64:]
    cross = full[:TR, TR:]
    cross = 0.5 * (cross + full[TR:, :TR])
    rhs, images = full[:TR, :TR], full[TR:, TR:]
    row, col = places()
    diagonal = jnp.sum(jnp.where(row == col, images, 0.0), axis=0, keepdims=True)
    first = jnp.where(row >= col, rhs, images)
    second = jnp.where(row == 0, diagonal, images[:1, :1])
    gram_ref[0:8, :] = lay_flat(first)
    gram_ref[8:16, :] = lay_flat(jnp.where(row >= col, cross, second))


def grams(own, near, far, highs, lows, right):
    return pl.pallas_call(
        gram_kernel,
        out_shape=(shape((TR, NODE_DEV)), shape((16, 128))),
        in_specs=vmem(6),
        out_specs=tuple(vmem(2)),
        scratch_shapes=[pltpu.VMEM((OWN_BLOCKS * 2 * TR, L), F32)],
        compiler_params=params(),
        name="grams",
    )(own, near, far, highs, lows, right)


def hdot(a, b, dims=(((1,), (0,)), ((), ()))):
    return lax.dot_general(a, b, dims, precision=lax.Precision.HIGHEST, preferred_element_type=F32)


def eliminate(work, above):
    groups = TR // 8
    row = lax.broadcasted_iota(jnp.int32, (8, 128), 0)
    work = [work[8 * g : 8 * g + 8] for g in range(groups)]
    scale = [jnp.zeros((8, 128), F32)] * groups
    for panel in range(groups):
        columns = {
            k: [jnp.broadcast_to(work[g][:, k : k + 1], (8, 128)) for g in range(groups)]
            for k in range(8 * panel, 8 * panel + 8)
        }
        for k in range(8 * panel, 8 * panel + 8):
            g0, r = divmod(k, 8)
            column = columns[k]
            pivot = column[g0][r : r + 1]
            inverse = 1.0 / pivot
            if not above:
                scale[g0] = jnp.where(row == r, jnp.broadcast_to(pivot, (8, 128)), scale[g0])

            def update(target):
                line = jnp.broadcast_to(target[g0][r : r + 1] * inverse, (8, 128))
                out = []
                for g in range(groups):
                    if g < g0 and not above:
                        out.append(target[g])
                    elif g == g0:
                        less = target[g] - column[g] * line
                        if above:
                            out.append(jnp.where(row == r, line, less))
                        else:
                            out.append(jnp.where(row > r, less, target[g]))
                    else:
                        out.append(target[g] - column[g] * line)
                return out

            work = update(work)
            for j in range(k + 1, 8 * panel + 8):
                columns[j] = update(columns[j])
    if not above:
        work = [w * lax.rsqrt(s) for w, s in zip(work, scale)]
    return jnp.concatenate(work, axis=0)


def final_kernel(gram_ref, right_ref, image_ref, sol_ref, res_ref, new_ref):
    total = gram_ref[0]
    for i in range(1, gram_ref.shape[0]):
        total = total + gram_ref[i]
    first = lay_square(total[:8])
    second = lay_square(total[8:])
    first_t = first.T
    second_t = second.T
    row, col = places()
    rhs = jnp.where(row >= col, first, first_t)
    cross = jnp.where(row >= col, second, second_t)
    diagonal = jnp.where(col == 0, second[1:2, 2:3], second[:1, :])
    images = jnp.where(row < col, first, jnp.where(row == col, diagonal, first_t))
    zero = jnp.zeros((TR, TR), F32)
    eye = jnp.where(row == col, 1.0, 0.0)

    weights_t = eliminate(jnp.concatenate([cross, rhs, zero, zero], axis=1), True)[:, TR : 2 * TR]
    weights = weights_t.T
    both = hdot(weights, jnp.concatenate([cross, images], axis=1))
    gram = rhs - 2.0 * both[:, :TR] + hdot(both[:, TR:], weights_t)
    work = eliminate(jnp.concatenate([gram, eye, weights, zero], axis=1), False)
    inverse = work[:, TR : 2 * TR]
    mixed = work[:, 2 * TR : 3 * TR]
    coeffs = jnp.concatenate(
        [
            jnp.concatenate([weights, zero], axis=1),
            jnp.concatenate([zero, -weights], axis=1),
            jnp.concatenate([inverse, -mixed], axis=1),
        ],
        axis=0,
    )
    high, low = split2(coeffs)
    right = right_ref[...]
    rh, rl = split2(right)
    ih, il = split2(image_ref[...])
    highs = jnp.concatenate([rh, ih], axis=0)
    lows = jnp.concatenate([rl, il], axis=0)
    out = (
        jnp.dot(high, highs, preferred_element_type=F32)
        + jnp.dot(high, lows, preferred_element_type=F32)
        + jnp.dot(low, highs, preferred_element_type=F32)
    )
    sol_ref[...] = out[:TR]
    res_ref[...] = right + out[TR : 2 * TR]
    new_ref[...] = out[2 * TR :]


def finish(gram, right, image):
    return pl.pallas_call(
        final_kernel,
        out_shape=(shape((TR, NODE_DEV)),) * 3,
        in_specs=vmem(3),
        out_specs=tuple(vmem(3)),
        compiler_params=params(),
        name="finish",
    )(gram, right, image)


def swapped(near, far):
    outer = [(i, j) for k in range(1, 511, 2) for i, j in ((k, k + 1), (k + 1, k))]
    far = lax.ppermute(far, AXES, outer)
    near = lax.ppermute(near, AXES, [(i, i ^ 1) for i in range(512)])
    return near, far


def exchanged(value, axes):
    count = int(np.prod([SIZES[a] for a in axes]))
    copies = lax.optimization_barrier(jnp.broadcast_to(value[None], (count,) + value.shape))
    return lax.all_to_all(copies, axes, 0, 0)


def per_device(connectivity, send_down, send_up, jacobian, pair_blocks, pair_target, pair_source, source_values):
    lows = send_down
    highs = send_up
    mass = jnp.asarray(mass_tiles())
    ids, parts, near, far = right_side_halo(pair_target, pair_source, connectivity.T, pair_blocks, source_values)
    near, far = swapped(near, far)
    own = scatter_own_first(parts)
    right, near, far, table = settle_right(own, near, far, highs, lows)
    near, far = swapped(near, far)
    start, scale = gather_own(ids, table, jacobian[None, :])
    parts, near, far = mass_halo(ids, start, near, far, scale, mass)
    near, far = swapped(near, far)
    own = scatter_own(ids, parts)
    image, gram = grams(own, near, far, highs, lows, right)
    gram = exchanged(gram, ("x", "y")).sum(0)
    gram = exchanged(gram, ("z", "c"))
    return finish(gram, right, image)


def solution(mesh):
    mesh = Mesh(mesh.devices.reshape(4, 8, 8, 2), AXES)
    return jax.shard_map(
        per_device,
        mesh=mesh,
        in_specs=(
            P(AXES, None),
            P(AXES, None),
            P(AXES, None),
            P(AXES),
            P(AXES, None),
            P(AXES),
            P(AXES),
            P(None, AXES),
        ),
        out_specs=(P(None, AXES), P(None, AXES), P(None, AXES)),
        check_vma=False,
    )
```

```python
import jax
import jax.numpy as jnp
import numpy as np
from jax import lax
from jax.experimental import pallas as pl
from jax.experimental.pallas import tpu as pltpu
from jax.sharding import Mesh
from jax.sharding import PartitionSpec as P

TR = 32
NODE_DEV = 3456
F = 768
SLOTS = 8192
L = 512
OWN_BLOCKS = 7
HALO = 256
HALO_FIRST = OWN_BLOCKS * L // HALO
HALO_BLOCKS = 6
PAD = OWN_BLOCKS * L - NODE_DEV
BF = jnp.bfloat16
F32 = jnp.float32
I16 = jnp.int16
NT = (((1,), (1,)), ((), ()))
AXES = ("x", "z", "y", "c")
SIZES = {"x": 4, "z": 8, "y": 8, "c": 2}

line_mass = (
    np.array(
        [
            [128.0, 99.0, -36.0, 19.0],
            [99.0, 648.0, -81.0, -36.0],
            [-36.0, -81.0, 648.0, 99.0],
            [19.0, -36.0, 99.0, 128.0],
        ]
    )
    / 504.0
)
mass_table = np.kron(np.kron(line_mass, line_mass), line_mass)


def mass_tiles():
    order = np.arange(64).reshape(32, 2).T.reshape(-1)
    block = mass_table[np.ix_(order, order)].astype(np.float32)
    whole = np.kron(np.eye(4, dtype=np.float32), block)
    high = whole.astype(jnp.bfloat16)
    low = (whole - high.astype(np.float32)).astype(jnp.bfloat16)
    return np.concatenate([high, low], axis=1)


def params(mebibytes=24):
    return pltpu.CompilerParams(vmem_limit_bytes=mebibytes * 2**20)


def vmem(count):
    return [pl.BlockSpec(memory_space=pltpu.VMEM)] * count


def hbm(count):
    return [pl.BlockSpec(memory_space=pltpu.MemorySpace.HBM)] * count


def shape(dims, kind=F32):
    return jax.ShapeDtypeStruct(dims, kind)


def aligned(start, size):
    return pl.ds(pl.multiple_of(start, size), size)


def split2(value):
    high = value.astype(BF)
    low = (value - high.astype(F32)).astype(BF)
    return high, low


def one_hot(row, size=L):
    spread = jnp.broadcast_to(row.astype(I16), (size, 128))
    index = lax.broadcasted_iota(I16, (size, 128), 0)
    return jnp.where(spread == index, jnp.ones((), BF), jnp.zeros((), BF))


def tiles_of(ids, count, size=L):
    blocks = lax.shift_right_logical(ids, size.bit_length() - 1)
    places = ids & (size - 1)
    hot = jnp.concatenate([one_hot(places[j : j + 1], size) for j in range(count)], axis=1)
    return hot, [blocks[j : j + 1] for j in range(count)]


def masked(parts, blocks, first, number):
    out = []
    for j, row in enumerate(blocks):
        here = jnp.broadcast_to(row.astype(I16), (2 * TR, 128))
        tile = parts[:, j * 128 : (j + 1) * 128]
        out.append(
            jnp.concatenate(
                [jnp.where(here == first + b, tile, jnp.zeros((), BF)) for b in range(number)], axis=0
            )
        )
    return jnp.concatenate(out, axis=1)


def picked(rows, blocks, first, number, start):
    out = []
    for j, row in enumerate(blocks):
        tile = start[j]
        height = tile.shape[0]
        here = jnp.broadcast_to(row, (height, 128))
        for b in range(number):
            tile = jnp.where(here == first + b, rows[b * height : (b + 1) * height, j * 128 : (j + 1) * 128], tile)
        out.append(tile)
    return out


def add_scatter(acc, parts, ids, count, first, number, size=L):
    hot, blocks = tiles_of(ids, count, size)
    acc[...] += lax.dot_general(
        masked(parts, blocks, first, number), hot, NT, preferred_element_type=F32
    )


def fold(acc, b):
    return acc[b * 2 * TR : b * 2 * TR + TR] + acc[b * 2 * TR + TR : (b + 1) * 2 * TR]


CHUNK = 2048
TILES = CHUNK // 128
UNROLL = 128


def rhs_kernel(
    tgt_hbm,
    src_hbm,
    conn_hbm,
    pb_hbm,
    sv_hbm,
    ids_hbm,
    parts_hbm,
    near_ref,
    far_ref,
    tgt_ref,
    src_ref,
    conn_ref,
    pb_ref,
    sv_ref,
    ids_ref,
    parts_ref,
    blocks,
    source,
    total,
    wide,
    acc,
    sems,
):
    zero = jnp.zeros((), F32)
    zero16 = jnp.zeros((), BF)
    small = [
        pltpu.make_async_copy(a, b, sems.at[i])
        for i, (a, b) in enumerate(((sv_hbm, sv_ref), (conn_hbm, conn_ref), (tgt_hbm, tgt_ref), (src_hbm, src_ref)))
    ]
    large = [
        pltpu.make_async_copy(pb_hbm.at[pl.ds(64 * i, 64), :], pb_ref.at[pl.ds(64 * i, 64), :], sems.at[4 + i]) for i in range(4)
    ]
    for copy in small + large:
        copy.start()
    total[...] = jnp.zeros_like(total)
    small[0].wait()
    for g in range(16):
        stack = jnp.concatenate([sv_ref[:, (4 * g + k) * 128 : (4 * g + k + 1) * 128] for k in range(4)], axis=0)
        source[g * 128 : (g + 1) * 128, :] = stack.astype(F32).T.astype(BF)
    for copy in small[1:]:
        copy.wait()
    for i in range(4):
        large[i].wait()

        @pl.loop(4 * i, 4 * i + 4)
        def _(g):
            for c in range(32):
                rows = pb_ref[aligned(g * 16, 16), c * 128 : (c + 1) * 128].astype(F32)
                blocks[pl.ds(g * 528 + c, 16, stride=33), :] = rows

    conn = conn_ref[...].astype(F32).T.astype(jnp.int32)
    row = lax.broadcasted_iota(jnp.int32, (64, 64), 0)
    col = lax.broadcasted_iota(jnp.int32, (64, 64), 1)
    swap = jnp.where(row == 2 * (col & 31) + lax.shift_right_logical(col, 5), 1.0, 0.0).astype(BF)
    upper = lax.shift_right_logical(conn, 7).astype(F32).astype(BF)
    lower = (conn & 127).astype(F32).astype(BF)
    ids = jnp.dot(upper, swap, preferred_element_type=F32) * 128.0 + jnp.dot(lower, swap, preferred_element_type=F32)
    ids = ids.astype(jnp.int32)
    ids = jnp.where(ids >= NODE_DEV, ids + PAD, ids)
    wide[...] = jnp.concatenate([ids, ids], axis=1)
    lane64 = lax.broadcasted_iota(jnp.int32, (64, 128), 1)
    ids_ref[...] = jnp.where(lane64 < 64, wide[pl.ds(0, 64, stride=2), :], wide[pl.ds(1, 64, stride=2), :])

    low32 = lax.broadcasted_iota(jnp.int32, (32, 128), 1) < 64
    group = lax.shift_right_logical(lane64, 5).astype(I16)

    @pl.loop(0, 256 // UNROLL)
    def _(i):
        for u in range(UNROLL):
            p = i * UNROLL + u
            s = src_ref[p]
            e = tgt_ref[p]
            k = lax.shift_right_logical(s, 1) & 3
            start = lax.shift_right_logical(s, 3) * 128 + (s & 1) * 64
            value = jnp.where(group == k.astype(I16), source[aligned(start, 64), :], zero16)
            block = blocks[pl.ds(p * 33,32), :]
            rows = jnp.concatenate([jnp.where(low32, block, zero), jnp.where(low32, zero, block)], axis=0).astype(BF)
            total[aligned(e * 64, 64), :] += jnp.dot(
                rows, jnp.concatenate([value, value], axis=0), preferred_element_type=F32
            )

    lanes = lax.shift_right_logical(lax.broadcasted_iota(jnp.int32, (128, 128), 1), 5)
    odd = (lanes & 1) == 1
    up = lanes >= 2

    def join(a, b, mask, by):
        return jnp.where(mask, b, a) + pltpu.roll(jnp.where(mask, a, b), by, 1)

    results = [pltpu.make_async_copy(ids_ref, ids_hbm, sems.at[8])] + [
        pltpu.make_async_copy(
            parts_ref.at[:, pl.ds(i * CHUNK, CHUNK)], parts_hbm.at[:, pl.ds(i * CHUNK, CHUNK)], sems.at[9 + i]
        )
        for i in range(SLOTS // CHUNK)
    ]
    results[0].start()
    for g in range(16):
        e = [total[aligned(g * 512 + j * 128, 128), :] for j in range(4)]
        both = join(join(e[0], e[1], odd, 32), join(e[2], e[3], odd, 32), up, 64).T
        for j in range(4):
            high, low = split2(both[j * TR : (j + 1) * TR])
            parts_ref[:, aligned(g * 512 + j * 128, 128)] = jnp.concatenate([high, low, id_rows(ids_ref[pl.ds(4 * g + j, 1), :])], axis=0)
        if g % 4 == 3:
            results[1 + g // 4].start()

    scatter_halo(ids_ref, parts_ref, acc)
    halves(acc, near_ref, far_ref)
    for copy in results:
        copy.wait()


def id_rows(ids):
    row = lax.broadcasted_iota(jnp.int32, (16, 128), 0)
    ids = jnp.broadcast_to(ids, (16, 128))
    block = lax.shift_right_logical(ids, 9)
    half = lax.shift_right_logical(ids, 8) & 1
    return jnp.where(row == 0, block, jnp.where(row == 1, half, ids & 255)).astype(F32).astype(BF)


def own_first_kernel(parts_hbm, out_ref, parts_ref, acc, sems):
    copies = [
        pltpu.make_async_copy(
            parts_hbm.at[:, pl.ds(k * CHUNK, CHUNK)], parts_ref.at[:, pl.ds(k * CHUNK, CHUNK)], sems.at[k]
        )
        for k in range(SLOTS // CHUNK)
    ]
    for copy in copies:
        copy.start()
    acc[...] = jnp.zeros_like(acc)
    for k, copy in enumerate(copies):
        copy.wait()
        rows = [parts_ref[2 * TR :, k * CHUNK + j * 128 : k * CHUNK + (j + 1) * 128].astype(F32) for j in range(TILES)]
        hot = jnp.concatenate([one_hot((r[1:2] * 256.0 + r[2:3]).astype(jnp.int32)) for r in rows], axis=1)
        blocks = [r[0:1].astype(jnp.int32) for r in rows]
        parts = masked(parts_ref[: 2 * TR, k * CHUNK : (k + 1) * CHUNK], blocks, 0, OWN_BLOCKS)
        acc[...] += lax.dot_general(parts, hot, NT, preferred_element_type=F32)
    for b in range(OWN_BLOCKS):
        out_ref[:, b * L : (b + 1) * L] = fold(acc, b)


def scatter_own_first(parts):
    return pl.pallas_call(
        own_first_kernel,
        out_shape=shape((TR, OWN_BLOCKS * L)),
        in_specs=hbm(1),
        out_specs=vmem(1)[0],
        scratch_shapes=[
            pltpu.VMEM((2 * TR + 16, SLOTS), BF),
            pltpu.VMEM((OWN_BLOCKS * 2 * TR, L), F32),
            pltpu.SemaphoreType.DMA((SLOTS // CHUNK,)),
        ],
        compiler_params=pltpu.CompilerParams(vmem_limit_bytes=54784 * 2**10),
        cost_estimate=pl.CostEstimate(flops=2 * 448 * 512 * 8192, bytes_accessed=2**21, transcendentals=0),
        name="own_first",
    )(parts)


def scatter_halo(ids_ref, parts_ref, acc):
    acc[...] = jnp.zeros_like(acc)

    @pl.loop(0, SLOTS // CHUNK, unroll=True)
    def _(k):
        add_scatter(
            acc,
            parts_ref[: 2 * TR, aligned(k * CHUNK, CHUNK)],
            ids_ref[aligned(k * TILES, TILES), :],
            TILES,
            HALO_FIRST,
            HALO_BLOCKS,
            HALO,
        )


def upper_first():
    return lax.axis_index("c") == 0


def halves(acc, near_ref, far_ref):
    half = HALO_BLOCKS // 2
    low, high = (jnp.concatenate([fold(acc, b) for b in range(i, i + half)], axis=1) for i in (0, half))
    upward = upper_first()
    near_ref[...] = jnp.where(upward, high, low)
    far_ref[...] = jnp.where(upward, low, high)


def arrived(near_ref, far_ref):
    upward = upper_first()
    near, far = near_ref[...], far_ref[...]
    return jnp.where(upward, near, far), jnp.where(upward, far, near)


def right_side_halo(tgt, src, conn, pair_blocks, source_values):
    return pl.pallas_call(
        rhs_kernel,
        out_shape=(shape((64, 128), jnp.int32), shape((2 * TR + 16, SLOTS), BF), shape((TR, F)), shape((TR, F))),
        in_specs=hbm(5),
        out_specs=tuple(hbm(2) + vmem(2)),
        scratch_shapes=[
            pltpu.SMEM((256,), jnp.int32),
            pltpu.SMEM((256,), jnp.int32),
            pltpu.VMEM((64, 128), jnp.int32),
            pltpu.VMEM((256, 4096), BF),
            pltpu.VMEM((TR, SLOTS), BF),
            pltpu.VMEM((64, 128), jnp.int32),
            pltpu.VMEM((2 * TR + 16, SLOTS), BF),
            pltpu.VMEM((8448, 128), F32),
            pltpu.VMEM((2048, 128), BF),
            pltpu.VMEM((8192, 128), F32),
            pltpu.VMEM((128, 128), jnp.int32),
            pltpu.VMEM((HALO_BLOCKS * 2 * TR, HALO), F32),
            pltpu.SemaphoreType.DMA((9 + SLOTS // CHUNK,)),
        ],
        compiler_params=params(54),
        name="rhs",
    )(tgt, src, conn, pair_blocks, source_values)


def own_kernel(ids_ref, parts_ref, out_ref, acc):
    acc[...] = jnp.zeros_like(acc)

    @pl.loop(0, SLOTS // CHUNK, unroll=True)
    def _(k):
        add_scatter(acc, parts_ref[:, aligned(k * CHUNK, CHUNK)], ids_ref[aligned(k * TILES, TILES), :], TILES, 0, OWN_BLOCKS)

    for b in range(OWN_BLOCKS):
        out_ref[:, b * L : (b + 1) * L] = fold(acc, b)


def scatter_own(ids, parts):
    return pl.pallas_call(
        own_kernel,
        out_shape=shape((TR, OWN_BLOCKS * L)),
        in_specs=vmem(2),
        out_specs=vmem(1)[0],
        scratch_shapes=[pltpu.VMEM((OWN_BLOCKS * 2 * TR, L), F32)],
        compiler_params=params(),
        cost_estimate=pl.CostEstimate(flops=2 * 448 * 512 * 8192, bytes_accessed=2**21, transcendentals=0),
        name="own",
    )(ids, parts)


def settle(own_ref, near_ref, far_ref, highs_ref, lows_ref, acc):
    rows = [highs_ref[:, j * 128 : (j + 1) * 128] for j in range(6)] + [lows_ref[:, j * 128 : (j + 1) * 128] for j in range(6)]
    hot = jnp.concatenate([one_hot(r & (L - 1)) for r in rows], axis=1)
    blocks = [lax.shift_right_logical(r, L.bit_length() - 1) for r in rows]
    high, low = split2(jnp.concatenate(arrived(near_ref, far_ref), axis=1))
    parts = jnp.concatenate([high, low], axis=0)
    acc[...] = lax.dot_general(masked(parts, blocks, 0, OWN_BLOCKS), hot, NT, preferred_element_type=F32)
    whole = [own_ref[:, b * L : (b + 1) * L] + fold(acc, b) for b in range(OWN_BLOCKS)]
    return whole, hot, blocks


def settle_kernel(own_ref, near_ref, far_ref, highs_ref, lows_ref, out_ref, near_out, far_out, table_ref, acc):
    whole, hot, blocks = settle(own_ref, near_ref, far_ref, highs_ref, lows_ref, acc)
    for b, value in enumerate(whole):
        end = min(NODE_DEV, (b + 1) * L)
        out_ref[:, b * L : end] = value[:, : end - b * L]
        high, low = split2(value)
        table_ref[b * TR : (b + 1) * TR, :] = jnp.concatenate([high, low], axis=1)
    rows = jnp.dot(table_ref[...], jnp.concatenate([hot, hot], axis=0), preferred_element_type=F32)
    zeros = [jnp.zeros((TR, 128), F32)] * 12
    values = picked(rows, blocks, 0, OWN_BLOCKS, zeros)
    upward = upper_first()
    for j in range(6):
        near_out[:, j * 128 : (j + 1) * 128] = jnp.where(upward, values[j], values[6 + j])
        far_out[:, j * 128 : (j + 1) * 128] = jnp.where(upward, values[6 + j], values[j])


def settle_right(own, near, far, highs, lows):
    return pl.pallas_call(
        settle_kernel,
        out_shape=(
            shape((TR, NODE_DEV)),
            shape((TR, F)),
            shape((TR, F)),
            shape((OWN_BLOCKS * TR, 2 * L), BF),
        ),
        in_specs=vmem(5),
        out_specs=tuple(vmem(4)),
        scratch_shapes=[pltpu.VMEM((OWN_BLOCKS * 2 * TR, L), F32)],
        compiler_params=params(),
        name="settle",
    )(own, near, far, highs, lows)


def gather_kernel(ids_ref, table_ref, jac_ref, out_ref, scale_ref, wide):
    wide[...] = jnp.broadcast_to(jac_ref[...], (128, 128)).T
    lane64 = lax.broadcasted_iota(jnp.int32, (64, 128), 1)
    scale_ref[...] = jnp.where(lane64 < 64, wide[pl.ds(0, 64, stride=2), :], wide[pl.ds(1, 64, stride=2), :])

    @pl.loop(0, SLOTS // CHUNK, unroll=True)
    def _(k):
        hot, blocks = tiles_of(ids_ref[aligned(k * TILES, TILES), :], TILES)
        rows = jnp.dot(table_ref[...], jnp.concatenate([hot, hot], axis=0), preferred_element_type=F32)
        values = picked(rows, blocks, 0, OWN_BLOCKS, [jnp.zeros((TR, 128), F32)] * TILES)
        out_ref[:, aligned(k * CHUNK, CHUNK)] = jnp.concatenate(values, axis=1)


def gather_own(ids, table, jac):
    return pl.pallas_call(
        gather_kernel,
        out_shape=(shape((TR, SLOTS)), shape((64, 128))),
        in_specs=vmem(3),
        out_specs=tuple(vmem(2)),
        scratch_shapes=[pltpu.VMEM((128, 128), F32)],
        compiler_params=params(),
        cost_estimate=pl.CostEstimate(flops=2 * 448 * 512 * 8192, bytes_accessed=2**21, transcendentals=0),
        name="gather",
    )(ids, table, jac)


def mass_kernel(ids_ref, start_ref, near_ref, far_ref, scale_ref, mass_ref, parts_ref, near_out, far_out, table, acc):
    above, below = arrived(near_ref, far_ref)
    both = jnp.concatenate([below, above], axis=1)
    for b in range(HALO_BLOCKS):
        high, low = split2(both[:, b * HALO : (b + 1) * HALO])
        table[b * 2 * TR : (b + 1) * 2 * TR, :] = jnp.concatenate([high, low], axis=0)
    acc[...] = jnp.zeros_like(acc)

    @pl.loop(0, SLOTS // CHUNK, unroll=True)
    def _(k):
        hot, blocks = tiles_of(ids_ref[aligned(k * TILES, TILES), :], TILES, HALO)
        rows = jnp.dot(table[...], hot, preferred_element_type=F32)
        zeros = [jnp.zeros((2 * TR, 128), F32)] * TILES
        found = picked(rows, blocks, HALO_FIRST, HALO_BLOCKS, zeros)
        values = [
            start_ref[:, aligned(k * CHUNK + j * 128, 128)] + found[j][:TR] + found[j][TR:] for j in range(TILES)
        ]
        split = [split2(jnp.concatenate(values[2 * j : 2 * j + 2], axis=1)) for j in range(TILES // 2)]
        highs = jnp.concatenate([s[0] for s in split], axis=0)
        lows = jnp.concatenate([s[1] for s in split], axis=0)
        image = (
            jnp.dot(highs, mass_ref[:, :256], preferred_element_type=F32)
            + jnp.dot(lows, mass_ref[:, :256], preferred_element_type=F32)
            + jnp.dot(highs, mass_ref[:, 256:], preferred_element_type=F32)
        )
        tiles = []
        scales = scale_ref[aligned(k * TILES, TILES), :]
        for j in range(TILES):
            tile = image[(j // 2) * TR : (j // 2 + 1) * TR, (j % 2) * 128 : (j % 2 + 1) * 128]
            high, low = split2(tile * scales[j : j + 1])
            tiles.append(jnp.concatenate([high, low], axis=0))
        parts = jnp.concatenate(tiles, axis=1)
        parts_ref[:, aligned(k * CHUNK, CHUNK)] = parts
        acc[...] += lax.dot_general(
            masked(parts, blocks, HALO_FIRST, HALO_BLOCKS), hot, NT, preferred_element_type=F32
        )

    halves(acc, near_out, far_out)


def mass_halo(ids, start, near, far, scale, mass):
    return pl.pallas_call(
        mass_kernel,
        out_shape=(shape((2 * TR, SLOTS), BF), shape((TR, F)), shape((TR, F))),
        in_specs=vmem(6),
        out_specs=tuple(vmem(3)),
        scratch_shapes=[
            pltpu.VMEM((HALO_BLOCKS * 2 * TR, HALO), BF),
            pltpu.VMEM((HALO_BLOCKS * 2 * TR, HALO), F32),
        ],
        compiler_params=params(),
        name="mass",
    )(ids, start, near, far, scale, mass)


def places():
    return tuple(lax.broadcasted_iota(jnp.int32, (TR, TR), i) for i in range(2))


def lay_flat(square):
    return jnp.concatenate([square[8 * i : 8 * i + 8] for i in range(4)], axis=1)


def lay_square(flat):
    return jnp.concatenate([flat[:, 32 * i : 32 * i + 32] for i in range(4)], axis=0)


def gram_kernel(own_ref, near_ref, far_ref, highs_ref, lows_ref, right_ref, out_ref, gram_ref, acc):
    whole, _, _ = settle(own_ref, near_ref, far_ref, highs_ref, lows_ref, acc)
    for b, value in enumerate(whole):
        end = min(NODE_DEV, (b + 1) * L)
        out_ref[:, b * L : end] = value[:, : end - b * L]
    right = split2(right_ref[...])
    image = split2(out_ref[...])
    stack = jnp.concatenate([right[0], image[0], right[1], image[1]], axis=0)
    full = lax.dot_general(stack, stack, NT, preferred_element_type=F32)
    full = full[:64] + full[64:]
    full = full[:, :64] + full[:, 64:]
    cross = full[:TR, TR:]
    cross = 0.5 * (cross + full[TR:, :TR])
    rhs, images = full[:TR, :TR], full[TR:, TR:]
    row, col = places()
    diagonal = jnp.sum(jnp.where(row == col, images, 0.0), axis=0, keepdims=True)
    first = jnp.where(row >= col, rhs, images)
    second = jnp.where(row == 0, diagonal, images[:1, :1])
    gram_ref[0:8, :] = lay_flat(first)
    gram_ref[8:16, :] = lay_flat(jnp.where(row >= col, cross, second))


def grams(own, near, far, highs, lows, right):
    return pl.pallas_call(
        gram_kernel,
        out_shape=(shape((TR, NODE_DEV)), shape((16, 128))),
        in_specs=vmem(6),
        out_specs=tuple(vmem(2)),
        scratch_shapes=[pltpu.VMEM((OWN_BLOCKS * 2 * TR, L), F32)],
        compiler_params=params(),
        name="grams",
    )(own, near, far, highs, lows, right)


def hdot(a, b, dims=(((1,), (0,)), ((), ()))):
    return lax.dot_general(a, b, dims, precision=lax.Precision.HIGHEST, preferred_element_type=F32)


def eliminate(work, above):
    groups = TR // 8
    row = lax.broadcasted_iota(jnp.int32, (8, 128), 0)
    work = [work[8 * g : 8 * g + 8] for g in range(groups)]
    scale = [jnp.zeros((8, 128), F32)] * groups
    for panel in range(groups):
        columns = {
            k: [jnp.broadcast_to(work[g][:, k : k + 1], (8, 128)) for g in range(groups)]
            for k in range(8 * panel, 8 * panel + 8)
        }
        for k in range(8 * panel, 8 * panel + 8):
            g0, r = divmod(k, 8)
            column = columns[k]
            pivot = column[g0][r : r + 1]
            inverse = 1.0 / pivot
            if not above:
                scale[g0] = jnp.where(row == r, jnp.broadcast_to(pivot, (8, 128)), scale[g0])

            def update(target):
                line = jnp.broadcast_to(target[g0][r : r + 1] * inverse, (8, 128))
                out = []
                for g in range(groups):
                    if g < g0 and not above:
                        out.append(target[g])
                    elif g == g0:
                        less = target[g] - column[g] * line
                        if above:
                            out.append(jnp.where(row == r, line, less))
                        else:
                            out.append(jnp.where(row > r, less, target[g]))
                    else:
                        out.append(target[g] - column[g] * line)
                return out

            work = update(work)
            for j in range(k + 1, 8 * panel + 8):
                columns[j] = update(columns[j])
    if not above:
        work = [w * lax.rsqrt(s) for w, s in zip(work, scale)]
    return jnp.concatenate(work, axis=0)


def final_kernel(gram_ref, right_ref, image_ref, sol_hbm, res_hbm, new_hbm, sol_ref, res_ref, new_ref, sems):
    outs = [
        pltpu.make_async_copy(a, b, sems.at[i])
        for i, (a, b) in enumerate(((sol_ref, sol_hbm), (res_ref, res_hbm), (new_ref, new_hbm)))
    ]
    right = right_ref[...]
    rh, rl = split2(right)
    ih, il = split2(image_ref[...])
    highs = jnp.concatenate([rh, ih], axis=0)
    lows = jnp.concatenate([rl, il], axis=0)

    def combine(coeffs):
        high, low = split2(coeffs)
        return (
            jnp.dot(high, highs, preferred_element_type=F32)
            + jnp.dot(high, lows, preferred_element_type=F32)
            + jnp.dot(low, highs, preferred_element_type=F32)
        )

    total = gram_ref[0]
    for i in range(1, gram_ref.shape[0]):
        total = total + gram_ref[i]
    first = lay_square(total[:8])
    second = lay_square(total[8:])
    first_t = first.T
    second_t = second.T
    row, col = places()
    rhs = jnp.where(row >= col, first, first_t)
    cross = jnp.where(row >= col, second, second_t)
    diagonal = jnp.where(col == 0, second[1:2, 2:3], second[:1, :])
    images = jnp.where(row < col, first, jnp.where(row == col, diagonal, first_t))
    zero = jnp.zeros((TR, TR), F32)
    eye = jnp.where(row == col, 1.0, 0.0)

    weights_t = eliminate(jnp.concatenate([cross, rhs, zero, zero], axis=1), True)[:, TR : 2 * TR]
    weights = weights_t.T
    out = combine(
        jnp.concatenate([jnp.concatenate([weights, zero], axis=1), jnp.concatenate([zero, -weights], axis=1)], axis=0)
    )
    sol_ref[...] = out[:TR]
    res_ref[...] = right + out[TR:]
    outs[0].start()
    outs[1].start()
    both = hdot(weights, jnp.concatenate([cross, images], axis=1))
    gram = rhs - 2.0 * both[:, :TR] + hdot(both[:, TR:], weights_t)
    work = eliminate(jnp.concatenate([gram, eye, weights, zero], axis=1), False)
    inverse = work[:, TR : 2 * TR]
    mixed = work[:, 2 * TR : 3 * TR]
    new_ref[...] = combine(jnp.concatenate([inverse, -mixed], axis=1))
    outs[2].start()
    for copy in outs:
        copy.wait()


def finish(gram, right, image):
    return pl.pallas_call(
        final_kernel,
        out_shape=(shape((TR, NODE_DEV)),) * 3,
        in_specs=vmem(3),
        out_specs=tuple(hbm(3)),
        scratch_shapes=[pltpu.VMEM((TR, NODE_DEV), F32)] * 3 + [pltpu.SemaphoreType.DMA((3,))],
        compiler_params=params(),
        name="finish",
    )(gram, right, image)


def swapped(near, far):
    outer = [(i, j) for k in range(1, 511, 2) for i, j in ((k, k + 1), (k + 1, k))]
    far = lax.ppermute(far, AXES, outer)
    near = lax.ppermute(near, AXES, [(i, i ^ 1) for i in range(512)])
    return near, far


def exchanged(value, axes):
    count = int(np.prod([SIZES[a] for a in axes]))
    copies = lax.optimization_barrier(jnp.broadcast_to(value[None], (count,) + value.shape))
    return lax.all_to_all(copies, axes, 0, 0)


def per_device(connectivity, send_down, send_up, jacobian, pair_blocks, pair_target, pair_source, source_values):
    lows = send_down
    highs = send_up
    mass = jnp.asarray(mass_tiles())
    ids, parts, near, far = right_side_halo(pair_target, pair_source, connectivity.T, pair_blocks, source_values)
    near, far = swapped(near, far)
    own = scatter_own_first(parts)
    right, near, far, table = settle_right(own, near, far, highs, lows)
    near, far = swapped(near, far)
    start, scale = gather_own(ids, table, jacobian[None, :])
    parts, near, far = mass_halo(ids, start, near, far, scale, mass)
    near, far = swapped(near, far)
    own = scatter_own(ids, parts)
    image, gram = grams(own, near, far, highs, lows, right)
    gram = exchanged(gram, ("x", "y")).sum(0)
    gram = exchanged(gram, ("z", "c"))
    return finish(gram, right, image)


def solution(mesh):
    mesh = Mesh(mesh.devices.reshape(4, 8, 8, 2), AXES)
    return jax.shard_map(
        per_device,
        mesh=mesh,
        in_specs=(
            P(AXES, None),
            P(AXES, None),
            P(AXES, None),
            P(AXES),
            P(AXES, None),
            P(AXES),
            P(AXES),
            P(None, AXES),
        ),
        out_specs=(P(None, AXES), P(None, AXES), P(None, AXES)),
        check_vma=False,
    )
```

```python
import jax
import jax.numpy as jnp
import numpy as np
from jax import lax
from jax.experimental import pallas as pl
from jax.experimental.pallas import tpu as pltpu
from jax.sharding import Mesh
from jax.sharding import PartitionSpec as P

TR = 32
NODE_DEV = 3456
F = 768
SLOTS = 8192
L = 512
OWN_BLOCKS = 7
HALO = 256
HALO_FIRST = OWN_BLOCKS * L // HALO
HALO_BLOCKS = 6
PAD = OWN_BLOCKS * L - NODE_DEV
BF = jnp.bfloat16
F32 = jnp.float32
I16 = jnp.int16
NT = (((1,), (1,)), ((), ()))
AXES = ("x", "z", "y", "c")
SIZES = {"x": 4, "z": 8, "y": 8, "c": 2}

line_mass = (
    np.array(
        [
            [128.0, 99.0, -36.0, 19.0],
            [99.0, 648.0, -81.0, -36.0],
            [-36.0, -81.0, 648.0, 99.0],
            [19.0, -36.0, 99.0, 128.0],
        ]
    )
    / 504.0
)
mass_table = np.kron(np.kron(line_mass, line_mass), line_mass)


def mass_tiles():
    order = np.arange(64).reshape(32, 2).T.reshape(-1)
    block = mass_table[np.ix_(order, order)].astype(np.float32)
    whole = np.kron(np.eye(4, dtype=np.float32), block)
    high = whole.astype(jnp.bfloat16)
    low = (whole - high.astype(np.float32)).astype(jnp.bfloat16)
    return np.concatenate([high, low], axis=1)


def params(mebibytes=24):
    return pltpu.CompilerParams(vmem_limit_bytes=mebibytes * 2**20)


def vmem(count):
    return [pl.BlockSpec(memory_space=pltpu.VMEM)] * count


def hbm(count):
    return [pl.BlockSpec(memory_space=pltpu.MemorySpace.HBM)] * count


def shape(dims, kind=F32):
    return jax.ShapeDtypeStruct(dims, kind)


def aligned(start, size):
    return pl.ds(pl.multiple_of(start, size), size)


def split2(value):
    high = value.astype(BF)
    low = (value - high.astype(F32)).astype(BF)
    return high, low


def one_hot(row, size=L):
    spread = jnp.broadcast_to(row.astype(I16), (size, 128))
    index = lax.broadcasted_iota(I16, (size, 128), 0)
    return jnp.where(spread == index, jnp.ones((), BF), jnp.zeros((), BF))


def tiles_of(ids, count, size=L):
    blocks = lax.shift_right_logical(ids, size.bit_length() - 1)
    places = ids & (size - 1)
    hot = jnp.concatenate([one_hot(places[j : j + 1], size) for j in range(count)], axis=1)
    return hot, [blocks[j : j + 1] for j in range(count)]


def masked(parts, blocks, first, number):
    out = []
    for j, row in enumerate(blocks):
        here = jnp.broadcast_to(row.astype(I16), (2 * TR, 128))
        tile = parts[:, j * 128 : (j + 1) * 128]
        out.append(
            jnp.concatenate(
                [jnp.where(here == first + b, tile, jnp.zeros((), BF)) for b in range(number)], axis=0
            )
        )
    return jnp.concatenate(out, axis=1)


def picked(rows, blocks, first, number, start):
    out = []
    for j, row in enumerate(blocks):
        tile = start[j]
        height = tile.shape[0]
        here = jnp.broadcast_to(row, (height, 128))
        for b in range(number):
            tile = jnp.where(here == first + b, rows[b * height : (b + 1) * height, j * 128 : (j + 1) * 128], tile)
        out.append(tile)
    return out


def add_scatter(acc, parts, ids, count, first, number, size=L):
    hot, blocks = tiles_of(ids, count, size)
    acc[...] += lax.dot_general(
        masked(parts, blocks, first, number), hot, NT, preferred_element_type=F32
    )


def fold(acc, b):
    return acc[b * 2 * TR : b * 2 * TR + TR] + acc[b * 2 * TR + TR : (b + 1) * 2 * TR]


CHUNK = 2048
TILES = CHUNK // 128
UNROLL = 64


def rhs_kernel(
    tgt_hbm,
    src_hbm,
    conn_hbm,
    pb_hbm,
    sv_hbm,
    ids_hbm,
    parts_hbm,
    near_ref,
    far_ref,
    tgt_ref,
    src_ref,
    conn_ref,
    pb_ref,
    sv_ref,
    ids_ref,
    parts_ref,
    blocks,
    source,
    total,
    wide,
    acc,
    sems,
):
    zero = jnp.zeros((), F32)
    zero16 = jnp.zeros((), BF)
    small = [
        pltpu.make_async_copy(a, b, sems.at[i])
        for i, (a, b) in enumerate(((sv_hbm, sv_ref), (conn_hbm, conn_ref), (tgt_hbm, tgt_ref), (src_hbm, src_ref)))
    ]
    large = [
        pltpu.make_async_copy(pb_hbm.at[pl.ds(64 * i, 64), :], pb_ref.at[pl.ds(64 * i, 64), :], sems.at[4 + i]) for i in range(4)
    ]
    for copy in small + large:
        copy.start()
    total[...] = jnp.zeros_like(total)
    small[0].wait()
    for g in range(16):
        stack = jnp.concatenate([sv_ref[:, (4 * g + k) * 128 : (4 * g + k + 1) * 128] for k in range(4)], axis=0)
        source[g * 128 : (g + 1) * 128, :] = stack.astype(F32).T.astype(BF)
    for copy in small[1:]:
        copy.wait()
    low32 = lax.broadcasted_iota(jnp.int32, (32, 128), 1) < 64
    group = lax.shift_right_logical(lax.broadcasted_iota(jnp.int32, (64, 128), 1), 5).astype(I16)

    @pl.loop(0, 256 // UNROLL)
    def _(i):
        pltpu.make_async_copy(pb_hbm.at[aligned(64 * i, 64), :], pb_ref.at[aligned(64 * i, 64), :], sems.at[4 + i]).wait()
        for q in range(4):
            for c in range(32):
                rows = pb_ref[aligned(i * 64 + q * 16, 16), c * 128 : (c + 1) * 128].astype(F32)
                blocks[pl.ds((i * 4 + q) * 528 + c, 16, stride=33), :] = rows
        for u in range(UNROLL):
            p = i * UNROLL + u
            s = src_ref[p]
            e = tgt_ref[p]
            k = lax.shift_right_logical(s, 1) & 3
            start = lax.shift_right_logical(s, 3) * 128 + (s & 1) * 64
            value = jnp.where(group == k.astype(I16), source[aligned(start, 64), :], zero16)
            block = blocks[pl.ds(p * 33,32), :]
            rows = jnp.concatenate([jnp.where(low32, block, zero), jnp.where(low32, zero, block)], axis=0).astype(BF)
            total[aligned(e * 64, 64), :] += jnp.dot(
                rows, jnp.concatenate([value, value], axis=0), preferred_element_type=F32
            )

    conn = conn_ref[...].astype(F32).T.astype(jnp.int32)
    row = lax.broadcasted_iota(jnp.int32, (64, 64), 0)
    col = lax.broadcasted_iota(jnp.int32, (64, 64), 1)
    swap = jnp.where(row == 2 * (col & 31) + lax.shift_right_logical(col, 5), 1.0, 0.0).astype(BF)
    upper = lax.shift_right_logical(conn, 7).astype(F32).astype(BF)
    lower = (conn & 127).astype(F32).astype(BF)
    ids = jnp.dot(upper, swap, preferred_element_type=F32) * 128.0 + jnp.dot(lower, swap, preferred_element_type=F32)
    ids = ids.astype(jnp.int32)
    ids = jnp.where(ids >= NODE_DEV, ids + PAD, ids)
    wide[...] = jnp.concatenate([ids, ids], axis=1)
    lane64 = lax.broadcasted_iota(jnp.int32, (64, 128), 1)
    ids_ref[...] = jnp.where(lane64 < 64, wide[pl.ds(0, 64, stride=2), :], wide[pl.ds(1, 64, stride=2), :])

    lanes = lax.shift_right_logical(lax.broadcasted_iota(jnp.int32, (128, 128), 1), 5)
    odd = (lanes & 1) == 1
    up = lanes >= 2

    def join(a, b, mask, by):
        return jnp.where(mask, b, a) + pltpu.roll(jnp.where(mask, a, b), by, 1)

    results = [pltpu.make_async_copy(ids_ref, ids_hbm, sems.at[8])] + [
        pltpu.make_async_copy(
            parts_ref.at[:, pl.ds(i * CHUNK, CHUNK)], parts_hbm.at[:, pl.ds(i * CHUNK, CHUNK)], sems.at[9 + i]
        )
        for i in range(SLOTS // CHUNK)
    ]
    results[0].start()
    for g in range(16):
        e = [total[aligned(g * 512 + j * 128, 128), :] for j in range(4)]
        both = join(join(e[0], e[1], odd, 32), join(e[2], e[3], odd, 32), up, 64).T
        for j in range(4):
            high, low = split2(both[j * TR : (j + 1) * TR])
            parts_ref[:, aligned(g * 512 + j * 128, 128)] = jnp.concatenate([high, low, id_rows(ids_ref[pl.ds(4 * g + j, 1), :])], axis=0)
        if g % 4 == 3:
            results[1 + g // 4].start()

    scatter_halo(ids_ref, parts_ref, acc)
    halves(acc, near_ref, far_ref)
    for copy in results:
        copy.wait()


def id_rows(ids):
    row = lax.broadcasted_iota(jnp.int32, (16, 128), 0)
    ids = jnp.broadcast_to(ids, (16, 128))
    block = lax.shift_right_logical(ids, 9)
    half = lax.shift_right_logical(ids, 8) & 1
    return jnp.where(row == 0, block, jnp.where(row == 1, half, ids & 255)).astype(F32).astype(BF)


def own_first_kernel(parts_hbm, out_ref, parts_ref, acc, sems):
    copies = [
        pltpu.make_async_copy(
            parts_hbm.at[:, pl.ds(k * CHUNK, CHUNK)], parts_ref.at[:, pl.ds(k * CHUNK, CHUNK)], sems.at[k]
        )
        for k in range(SLOTS // CHUNK)
    ]
    for copy in copies:
        copy.start()
    acc[...] = jnp.zeros_like(acc)
    for k, copy in enumerate(copies):
        copy.wait()
        rows = [parts_ref[2 * TR :, k * CHUNK + j * 128 : k * CHUNK + (j + 1) * 128].astype(F32) for j in range(TILES)]
        hot = jnp.concatenate([one_hot((r[1:2] * 256.0 + r[2:3]).astype(jnp.int32)) for r in rows], axis=1)
        blocks = [r[0:1].astype(jnp.int32) for r in rows]
        parts = masked(parts_ref[: 2 * TR, k * CHUNK : (k + 1) * CHUNK], blocks, 0, OWN_BLOCKS)
        acc[...] += lax.dot_general(parts, hot, NT, preferred_element_type=F32)
    for b in range(OWN_BLOCKS):
        out_ref[:, b * L : (b + 1) * L] = fold(acc, b)


def scatter_own_first(parts):
    return pl.pallas_call(
        own_first_kernel,
        out_shape=shape((TR, OWN_BLOCKS * L)),
        in_specs=hbm(1),
        out_specs=vmem(1)[0],
        scratch_shapes=[
            pltpu.VMEM((2 * TR + 16, SLOTS), BF),
            pltpu.VMEM((OWN_BLOCKS * 2 * TR, L), F32),
            pltpu.SemaphoreType.DMA((SLOTS // CHUNK,)),
        ],
        compiler_params=pltpu.CompilerParams(vmem_limit_bytes=54784 * 2**10),
        cost_estimate=pl.CostEstimate(flops=2 * 448 * 512 * 8192, bytes_accessed=2**21, transcendentals=0),
        name="own_first",
    )(parts)


def scatter_halo(ids_ref, parts_ref, acc):
    acc[...] = jnp.zeros_like(acc)

    @pl.loop(0, SLOTS // CHUNK, unroll=True)
    def _(k):
        add_scatter(
            acc,
            parts_ref[: 2 * TR, aligned(k * CHUNK, CHUNK)],
            ids_ref[aligned(k * TILES, TILES), :],
            TILES,
            HALO_FIRST,
            HALO_BLOCKS,
            HALO,
        )


def upper_first():
    return lax.axis_index("c") == 0


def halves(acc, near_ref, far_ref):
    half = HALO_BLOCKS // 2
    low, high = (jnp.concatenate([fold(acc, b) for b in range(i, i + half)], axis=1) for i in (0, half))
    upward = upper_first()
    near_ref[...] = jnp.where(upward, high, low)
    far_ref[...] = jnp.where(upward, low, high)


def arrived(near_ref, far_ref):
    upward = upper_first()
    near, far = near_ref[...], far_ref[...]
    return jnp.where(upward, near, far), jnp.where(upward, far, near)


def right_side_halo(tgt, src, conn, pair_blocks, source_values):
    return pl.pallas_call(
        rhs_kernel,
        out_shape=(shape((64, 128), jnp.int32), shape((2 * TR + 16, SLOTS), BF), shape((TR, F)), shape((TR, F))),
        in_specs=hbm(5),
        out_specs=tuple(hbm(2) + vmem(2)),
        scratch_shapes=[
            pltpu.SMEM((256,), jnp.int32),
            pltpu.SMEM((256,), jnp.int32),
            pltpu.VMEM((64, 128), jnp.int32),
            pltpu.VMEM((256, 4096), BF),
            pltpu.VMEM((TR, SLOTS), BF),
            pltpu.VMEM((64, 128), jnp.int32),
            pltpu.VMEM((2 * TR + 16, SLOTS), BF),
            pltpu.VMEM((8448, 128), F32),
            pltpu.VMEM((2048, 128), BF),
            pltpu.VMEM((8192, 128), F32),
            pltpu.VMEM((128, 128), jnp.int32),
            pltpu.VMEM((HALO_BLOCKS * 2 * TR, HALO), F32),
            pltpu.SemaphoreType.DMA((9 + SLOTS // CHUNK,)),
        ],
        compiler_params=params(54),
        name="rhs",
    )(tgt, src, conn, pair_blocks, source_values)


def own_kernel(ids_ref, parts_ref, out_ref, acc):
    acc[...] = jnp.zeros_like(acc)

    @pl.loop(0, SLOTS // CHUNK, unroll=True)
    def _(k):
        add_scatter(acc, parts_ref[:, aligned(k * CHUNK, CHUNK)], ids_ref[aligned(k * TILES, TILES), :], TILES, 0, OWN_BLOCKS)

    for b in range(OWN_BLOCKS):
        out_ref[:, b * L : (b + 1) * L] = fold(acc, b)


def scatter_own(ids, parts):
    return pl.pallas_call(
        own_kernel,
        out_shape=shape((TR, OWN_BLOCKS * L)),
        in_specs=vmem(2),
        out_specs=vmem(1)[0],
        scratch_shapes=[pltpu.VMEM((OWN_BLOCKS * 2 * TR, L), F32)],
        compiler_params=params(),
        cost_estimate=pl.CostEstimate(flops=2 * 448 * 512 * 8192, bytes_accessed=2**21, transcendentals=0),
        name="own",
    )(ids, parts)


def settle(own_ref, near_ref, far_ref, highs_ref, lows_ref, acc):
    rows = [highs_ref[:, j * 128 : (j + 1) * 128] for j in range(6)] + [lows_ref[:, j * 128 : (j + 1) * 128] for j in range(6)]
    hot = jnp.concatenate([one_hot(r & (L - 1)) for r in rows], axis=1)
    blocks = [lax.shift_right_logical(r, L.bit_length() - 1) for r in rows]
    high, low = split2(jnp.concatenate(arrived(near_ref, far_ref), axis=1))
    parts = jnp.concatenate([high, low], axis=0)
    acc[...] = lax.dot_general(masked(parts, blocks, 0, OWN_BLOCKS), hot, NT, preferred_element_type=F32)
    whole = [own_ref[:, b * L : (b + 1) * L] + fold(acc, b) for b in range(OWN_BLOCKS)]
    return whole, hot, blocks


def settle_kernel(own_ref, near_ref, far_ref, highs_ref, lows_ref, out_ref, near_out, far_out, table_ref, acc):
    whole, hot, blocks = settle(own_ref, near_ref, far_ref, highs_ref, lows_ref, acc)
    for b, value in enumerate(whole):
        end = min(NODE_DEV, (b + 1) * L)
        out_ref[:, b * L : end] = value[:, : end - b * L]
        high, low = split2(value)
        table_ref[b * TR : (b + 1) * TR, :] = jnp.concatenate([high, low], axis=1)
    rows = jnp.dot(table_ref[...], jnp.concatenate([hot, hot], axis=0), preferred_element_type=F32)
    zeros = [jnp.zeros((TR, 128), F32)] * 12
    values = picked(rows, blocks, 0, OWN_BLOCKS, zeros)
    upward = upper_first()
    for j in range(6):
        near_out[:, j * 128 : (j + 1) * 128] = jnp.where(upward, values[j], values[6 + j])
        far_out[:, j * 128 : (j + 1) * 128] = jnp.where(upward, values[6 + j], values[j])


def settle_right(own, near, far, highs, lows):
    return pl.pallas_call(
        settle_kernel,
        out_shape=(
            shape((TR, NODE_DEV)),
            shape((TR, F)),
            shape((TR, F)),
            shape((OWN_BLOCKS * TR, 2 * L), BF),
        ),
        in_specs=vmem(5),
        out_specs=tuple(vmem(4)),
        scratch_shapes=[pltpu.VMEM((OWN_BLOCKS * 2 * TR, L), F32)],
        compiler_params=params(),
        name="settle",
    )(own, near, far, highs, lows)


def gather_kernel(ids_ref, table_ref, jac_ref, out_ref, scale_ref, wide):
    wide[...] = jnp.broadcast_to(jac_ref[...], (128, 128)).T
    lane64 = lax.broadcasted_iota(jnp.int32, (64, 128), 1)
    scale_ref[...] = jnp.where(lane64 < 64, wide[pl.ds(0, 64, stride=2), :], wide[pl.ds(1, 64, stride=2), :])

    @pl.loop(0, SLOTS // CHUNK, unroll=True)
    def _(k):
        hot, blocks = tiles_of(ids_ref[aligned(k * TILES, TILES), :], TILES)
        rows = jnp.dot(table_ref[...], jnp.concatenate([hot, hot], axis=0), preferred_element_type=F32)
        values = picked(rows, blocks, 0, OWN_BLOCKS, [jnp.zeros((TR, 128), F32)] * TILES)
        out_ref[:, aligned(k * CHUNK, CHUNK)] = jnp.concatenate(values, axis=1)


def gather_own(ids, table, jac):
    return pl.pallas_call(
        gather_kernel,
        out_shape=(shape((TR, SLOTS)), shape((64, 128))),
        in_specs=vmem(3),
        out_specs=tuple(vmem(2)),
        scratch_shapes=[pltpu.VMEM((128, 128), F32)],
        compiler_params=params(),
        cost_estimate=pl.CostEstimate(flops=2 * 448 * 512 * 8192, bytes_accessed=2**21, transcendentals=0),
        name="gather",
    )(ids, table, jac)


def mass_kernel(ids_ref, start_ref, near_ref, far_ref, scale_ref, mass_ref, parts_ref, near_out, far_out, table, acc):
    above, below = arrived(near_ref, far_ref)
    both = jnp.concatenate([below, above], axis=1)
    for b in range(HALO_BLOCKS):
        high, low = split2(both[:, b * HALO : (b + 1) * HALO])
        table[b * 2 * TR : (b + 1) * 2 * TR, :] = jnp.concatenate([high, low], axis=0)
    acc[...] = jnp.zeros_like(acc)

    @pl.loop(0, SLOTS // CHUNK, unroll=True)
    def _(k):
        hot, blocks = tiles_of(ids_ref[aligned(k * TILES, TILES), :], TILES, HALO)
        rows = jnp.dot(table[...], hot, preferred_element_type=F32)
        zeros = [jnp.zeros((2 * TR, 128), F32)] * TILES
        found = picked(rows, blocks, HALO_FIRST, HALO_BLOCKS, zeros)
        values = [
            start_ref[:, aligned(k * CHUNK + j * 128, 128)] + found[j][:TR] + found[j][TR:] for j in range(TILES)
        ]
        split = [split2(jnp.concatenate(values[2 * j : 2 * j + 2], axis=1)) for j in range(TILES // 2)]
        highs = jnp.concatenate([s[0] for s in split], axis=0)
        lows = jnp.concatenate([s[1] for s in split], axis=0)
        image = (
            jnp.dot(highs, mass_ref[:, :256], preferred_element_type=F32)
            + jnp.dot(lows, mass_ref[:, :256], preferred_element_type=F32)
            + jnp.dot(highs, mass_ref[:, 256:], preferred_element_type=F32)
        )
        tiles = []
        scales = scale_ref[aligned(k * TILES, TILES), :]
        for j in range(TILES):
            tile = image[(j // 2) * TR : (j // 2 + 1) * TR, (j % 2) * 128 : (j % 2 + 1) * 128]
            high, low = split2(tile * scales[j : j + 1])
            tiles.append(jnp.concatenate([high, low], axis=0))
        parts = jnp.concatenate(tiles, axis=1)
        parts_ref[:, aligned(k * CHUNK, CHUNK)] = parts
        acc[...] += lax.dot_general(
            masked(parts, blocks, HALO_FIRST, HALO_BLOCKS), hot, NT, preferred_element_type=F32
        )

    halves(acc, near_out, far_out)


def mass_halo(ids, start, near, far, scale, mass):
    return pl.pallas_call(
        mass_kernel,
        out_shape=(shape((2 * TR, SLOTS), BF), shape((TR, F)), shape((TR, F))),
        in_specs=vmem(6),
        out_specs=tuple(vmem(3)),
        scratch_shapes=[
            pltpu.VMEM((HALO_BLOCKS * 2 * TR, HALO), BF),
            pltpu.VMEM((HALO_BLOCKS * 2 * TR, HALO), F32),
        ],
        compiler_params=params(),
        name="mass",
    )(ids, start, near, far, scale, mass)


def places():
    return tuple(lax.broadcasted_iota(jnp.int32, (TR, TR), i) for i in range(2))


def lay_flat(square):
    return jnp.concatenate([square[8 * i : 8 * i + 8] for i in range(4)], axis=1)


def lay_square(flat):
    return jnp.concatenate([flat[:, 32 * i : 32 * i + 32] for i in range(4)], axis=0)


def gram_kernel(own_ref, near_ref, far_ref, highs_ref, lows_ref, right_ref, out_ref, gram_ref, acc):
    whole, _, _ = settle(own_ref, near_ref, far_ref, highs_ref, lows_ref, acc)
    for b, value in enumerate(whole):
        end = min(NODE_DEV, (b + 1) * L)
        out_ref[:, b * L : end] = value[:, : end - b * L]
    right = split2(right_ref[...])
    image = split2(out_ref[...])
    stack = jnp.concatenate([right[0], image[0], right[1], image[1]], axis=0)
    full = lax.dot_general(stack, stack, NT, preferred_element_type=F32)
    full = full[:64] + full[64:]
    full = full[:, :64] + full[:, 64:]
    cross = full[:TR, TR:]
    cross = 0.5 * (cross + full[TR:, :TR])
    rhs, images = full[:TR, :TR], full[TR:, TR:]
    row, col = places()
    diagonal = jnp.sum(jnp.where(row == col, images, 0.0), axis=0, keepdims=True)
    first = jnp.where(row >= col, rhs, images)
    second = jnp.where(row == 0, diagonal, images[:1, :1])
    gram_ref[0:8, :] = lay_flat(first)
    gram_ref[8:16, :] = lay_flat(jnp.where(row >= col, cross, second))


def grams(own, near, far, highs, lows, right):
    return pl.pallas_call(
        gram_kernel,
        out_shape=(shape((TR, NODE_DEV)), shape((16, 128))),
        in_specs=vmem(6),
        out_specs=tuple(vmem(2)),
        scratch_shapes=[pltpu.VMEM((OWN_BLOCKS * 2 * TR, L), F32)],
        compiler_params=params(),
        name="grams",
    )(own, near, far, highs, lows, right)


def hdot(a, b, dims=(((1,), (0,)), ((), ()))):
    return lax.dot_general(a, b, dims, precision=lax.Precision.HIGHEST, preferred_element_type=F32)


def eliminate(work, above):
    groups = TR // 8
    row = lax.broadcasted_iota(jnp.int32, (8, 128), 0)
    work = [work[8 * g : 8 * g + 8] for g in range(groups)]
    scale = [jnp.zeros((8, 128), F32)] * groups
    for panel in range(groups):
        columns = {
            k: [jnp.broadcast_to(work[g][:, k : k + 1], (8, 128)) for g in range(groups)]
            for k in range(8 * panel, 8 * panel + 8)
        }
        for k in range(8 * panel, 8 * panel + 8):
            g0, r = divmod(k, 8)
            column = columns[k]
            pivot = column[g0][r : r + 1]
            inverse = 1.0 / pivot
            if not above:
                scale[g0] = jnp.where(row == r, jnp.broadcast_to(pivot, (8, 128)), scale[g0])

            def update(target):
                line = jnp.broadcast_to(target[g0][r : r + 1] * inverse, (8, 128))
                out = []
                for g in range(groups):
                    if g < g0 and not above:
                        out.append(target[g])
                    elif g == g0:
                        less = target[g] - column[g] * line
                        if above:
                            out.append(jnp.where(row == r, line, less))
                        else:
                            out.append(jnp.where(row > r, less, target[g]))
                    else:
                        out.append(target[g] - column[g] * line)
                return out

            work = update(work)
            for j in range(k + 1, 8 * panel + 8):
                columns[j] = update(columns[j])
    if not above:
        work = [w * lax.rsqrt(s) for w, s in zip(work, scale)]
    return jnp.concatenate(work, axis=0)


def final_kernel(gram_ref, right_ref, image_ref, sol_hbm, res_hbm, new_hbm, sol_ref, res_ref, new_ref, sems):
    outs = [
        pltpu.make_async_copy(a, b, sems.at[i])
        for i, (a, b) in enumerate(((sol_ref, sol_hbm), (res_ref, res_hbm), (new_ref, new_hbm)))
    ]
    right = right_ref[...]
    rh, rl = split2(right)
    ih, il = split2(image_ref[...])
    highs = jnp.concatenate([rh, ih], axis=0)
    lows = jnp.concatenate([rl, il], axis=0)

    def combine(coeffs):
        high, low = split2(coeffs)
        return (
            jnp.dot(high, highs, preferred_element_type=F32)
            + jnp.dot(high, lows, preferred_element_type=F32)
            + jnp.dot(low, highs, preferred_element_type=F32)
        )

    total = gram_ref[0]
    for i in range(1, gram_ref.shape[0]):
        total = total + gram_ref[i]
    first = lay_square(total[:8])
    second = lay_square(total[8:])
    first_t = first.T
    second_t = second.T
    row, col = places()
    rhs = jnp.where(row >= col, first, first_t)
    cross = jnp.where(row >= col, second, second_t)
    diagonal = jnp.where(col == 0, second[1:2, 2:3], second[:1, :])
    images = jnp.where(row < col, first, jnp.where(row == col, diagonal, first_t))
    zero = jnp.zeros((TR, TR), F32)
    eye = jnp.where(row == col, 1.0, 0.0)

    weights_t = eliminate(jnp.concatenate([cross, rhs, zero, zero], axis=1), True)[:, TR : 2 * TR]
    weights = weights_t.T
    out = combine(
        jnp.concatenate([jnp.concatenate([weights, zero], axis=1), jnp.concatenate([zero, -weights], axis=1)], axis=0)
    )
    sol_ref[...] = out[:TR]
    res_ref[...] = right + out[TR:]
    outs[0].start()
    outs[1].start()
    both = hdot(weights, jnp.concatenate([cross, images], axis=1))
    gram = rhs - 2.0 * both[:, :TR] + hdot(both[:, TR:], weights_t)
    work = eliminate(jnp.concatenate([gram, eye, weights, zero], axis=1), False)
    inverse = work[:, TR : 2 * TR]
    mixed = work[:, 2 * TR : 3 * TR]
    new_ref[...] = combine(jnp.concatenate([inverse, -mixed], axis=1))
    outs[2].start()
    for copy in outs:
        copy.wait()


def finish(gram, right, image):
    return pl.pallas_call(
        final_kernel,
        out_shape=(shape((TR, NODE_DEV)),) * 3,
        in_specs=vmem(3),
        out_specs=tuple(hbm(3)),
        scratch_shapes=[pltpu.VMEM((TR, NODE_DEV), F32)] * 3 + [pltpu.SemaphoreType.DMA((3,))],
        compiler_params=params(),
        name="finish",
    )(gram, right, image)


def swapped(near, far):
    outer = [(i, j) for k in range(1, 511, 2) for i, j in ((k, k + 1), (k + 1, k))]
    far = lax.ppermute(far, AXES, outer)
    near = lax.ppermute(near, AXES, [(i, i ^ 1) for i in range(512)])
    return near, far


def exchanged(value, axes):
    count = int(np.prod([SIZES[a] for a in axes]))
    copies = lax.optimization_barrier(jnp.broadcast_to(value[None], (count,) + value.shape))
    return lax.all_to_all(copies, axes, 0, 0)


def per_device(connectivity, send_down, send_up, jacobian, pair_blocks, pair_target, pair_source, source_values):
    lows = send_down
    highs = send_up
    mass = jnp.asarray(mass_tiles())
    ids, parts, near, far = right_side_halo(pair_target, pair_source, connectivity.T, pair_blocks, source_values)
    near, far = swapped(near, far)
    own = scatter_own_first(parts)
    right, near, far, table = settle_right(own, near, far, highs, lows)
    near, far = swapped(near, far)
    start, scale = gather_own(ids, table, jacobian[None, :])
    parts, near, far = mass_halo(ids, start, near, far, scale, mass)
    near, far = swapped(near, far)
    own = scatter_own(ids, parts)
    image, gram = grams(own, near, far, highs, lows, right)
    gram = exchanged(gram, ("x", "y")).sum(0)
    gram = exchanged(gram, ("z", "c"))
    return finish(gram, right, image)


def solution(mesh):
    mesh = Mesh(mesh.devices.reshape(4, 8, 8, 2), AXES)
    return jax.shard_map(
        per_device,
        mesh=mesh,
        in_specs=(
            P(AXES, None),
            P(AXES, None),
            P(AXES, None),
            P(AXES),
            P(AXES, None),
            P(AXES),
            P(AXES),
            P(None, AXES),
        ),
        out_specs=(P(None, AXES), P(None, AXES), P(None, AXES)),
        check_vma=False,
    )
```
